128 devices in a mesh: mode: 16 (over z_lo, x, core), mesh: 8 (over z_hi, y).
Axes of the slice: x: 4, y: 4, z: 4 (z_hi: 2, z_lo: 2; z = z_hi * 2 + z_lo), core: 2. Of those that a mesh axis runs over, the one named last changes fastest.
Arguments:
- velocity: float32 [3, 11, 11, 8, 32, 512], P(None, None, None, 'mesh', 'mode'), may hold values from -6 to 6
- penalty: float32 [11, 11, 8, 32], P(None, None, 'mesh'), may hold values from 0.5 to 8
Outputs:
- solution: float32 [512, 3, 11, 11, 8, 32], P('mode', None, None, None, 'mesh')
The draws below stay inside these ranges and needn't reach their ends.
All inputs are finite; a program needn't handle non-finite values.
Results may differ from the reference program's by a relative error of at most 0.0001.
Values sent between devices are 32-bit elements; how exact they have to be, the bound alone decides.
A program may use at most 256 MiB of HBM per device.

```python
import math
import jax
import jax.numpy as jnp
import numpy as np
from jax import lax

ORDER = 10
NQ = 11
PLANES = 512
MODES = 256
ITERS = 6
GX = 8
GY = 32


def block_scale(stream_key, shape, shards, low, high):
    gain = 1.0
    for position, shards_of in shards:
        draws = jax.random.uniform(jax.random.fold_in(jax.random.fold_in(stream_key, 6), position), (shards_of,), jnp.float32, low / len(shards), high / len(shards))
        gain = gain * jnp.repeat(jnp.exp(draws), shape[position] // shards_of).reshape((-1,) + (1,) * (len(shape) - 1 - position))
    return gain


def gaussian(key, dims, spread, reach, pieces=(), kind=jnp.bfloat16):
    factor_of = block_scale(key, dims, pieces, -0.22, 0.18) if pieces else 1.0
    drawn = jax.random.normal(key, dims, jnp.float32) * spread * factor_of
    return jnp.minimum(jnp.maximum(drawn, -reach), reach).astype(kind)


def setup_inputs(seed: int = 0) -> dict:
    streams_of = jax.random.split(jax.random.key(seed), 3)
    velocity = gaussian(streams_of[0], (3, NQ, NQ, GX, GY, PLANES), 1.0, 6.0, ((3, 8), (4, 16)), jnp.float32)
    penalty = jnp.clip(jnp.exp(math.log(8.0) - 2.7725887 * jax.random.uniform(streams_of[1], (NQ, NQ, GX, GY), jnp.float32) ** block_scale(streams_of[1], (NQ, NQ, GX, GY), ((2, 8),), -0.2, 0.2)), 0.5, 8.0)
    return dict(velocity=velocity, penalty=penalty)


helm_base = 1.0
span_wave = 0.02
bound_ratio = 25.0

def legendre_pair(points, order):
    previous = points * 0.0 + 1.0
    current = points * 1.0
    for degree in range(2, order + 1):
        following = ((2 * degree - 1) * points * current - (degree - 1) * previous) / degree
        previous = current
        current = following
    return (current, previous)

def gll_tables(order):
    count = order + 1
    points = -np.cos(np.pi * np.arange(count) / order)
    for sweep in range(200):
        top_vals, below_vals = legendre_pair(points, order)
        points = points - (points * top_vals - below_vals) / (count * top_vals)
    legendre_vals, below_vals = legendre_pair(points, order)
    weights = 2.0 / (order * (order + 1) * legendre_vals ** 2)
    identity = np.eye(count)
    spacing = points[:, None] - points[None, :] + identity
    derivative = legendre_vals[:, None] / (legendre_vals[None, :] * spacing) * (1.0 - identity)
    corner = np.concatenate([[-order * (order + 1) / 4.0], np.zeros(order - 1), [order * (order + 1) / 4.0]])
    derivative = derivative + identity * corner[None, :]
    stiffness = derivative.T @ (weights[:, None] * derivative)
    weight_mat = identity * weights[None, :]
    laplace = np.kron(stiffness, weight_mat) + np.kron(weight_mat, stiffness)
    upper_bound = float(np.max(np.sum(np.abs(laplace), axis=1) / np.sum(laplace * np.eye(count * count), axis=1)))
    weight_vec = jnp.asarray(weights, jnp.float32)
    stiff_mat = jnp.asarray(stiffness, jnp.float32)
    deriv_mat = jnp.asarray(derivative, jnp.float32)
    mass_two = weight_vec[:, None] * weight_vec[None, :]
    stiff_diag = jnp.diagonal(stiff_mat)
    lap_diag = stiff_diag[:, None] * weight_vec[None, :] + weight_vec[:, None] * stiff_diag[None, :]
    return (weight_vec, stiff_mat, deriv_mat, mass_two, lap_diag, upper_bound)

def advect(along_first, along_second, field, deriv_mat):
    grad_first = jnp.einsum('ia,...abxyz->...ibxyz', deriv_mat, field, precision=lax.Precision.HIGHEST)
    grad_second = jnp.einsum('jb,...abxyz->...ajxyz', deriv_mat, field, precision=lax.Precision.HIGHEST)
    return field - (along_first * grad_first + along_second * grad_second)

def make_coeff(first_row, count, penalty, mass_two):
    rows = (first_row + jnp.arange(count, dtype=jnp.int32)).astype(jnp.int32)
    wave = (rows % MODES).astype(jnp.float32)
    helm = helm_base + (span_wave * wave) ** 2
    return (helm[:, None, None, None, None, None] + penalty[None, None]) * mass_two[None, None, :, :, None, None]

def assemble(field, neighbours):
    top = field[:, :, :, -1]
    bottom = field[:, :, :, 0]
    shared = top[..., :-1] + bottom[..., 1:]
    top_new = jnp.concatenate([shared, top[..., -1:]], axis=-1)
    bottom_new = jnp.concatenate([bottom[..., :1], shared], axis=-1)
    field = field.at[:, :, :, -1].set(top_new).at[:, :, :, 0].set(bottom_new)
    right = field[:, :, -1]
    left = field[:, :, 0]
    shared = right[:, :, :, :-1] + left[:, :, :, 1:]
    from_lower, from_upper = neighbours(right[:, :, :, -1], left[:, :, :, 0])
    right_new = jnp.concatenate([shared, (right[:, :, :, -1] + from_upper)[:, :, :, None]], axis=3)
    left_new = jnp.concatenate([(left[:, :, :, 0] + from_lower)[:, :, :, None], shared], axis=3)
    return field.at[:, :, -1].set(right_new).at[:, :, 0].set(left_new)

def no_neighbours(right_edge, left_edge):
    return (jnp.zeros_like(right_edge), jnp.zeros_like(left_edge))

def helm_apply(field, coeff, stiff_mat, weight_vec):
    along_first = jnp.einsum('ia,rcabxy->rcibxy', stiff_mat, field, precision=lax.Precision.HIGHEST)
    along_second = jnp.einsum('jb,rcabxy->rcajxy', stiff_mat, field, precision=lax.Precision.HIGHEST)
    along_first = along_first * weight_vec[None, None, None, :, None, None]
    along_second = along_second * weight_vec[None, None, :, None, None, None]
    return along_first + along_second + coeff * field

def chebyshev(spectra, coeff, tables, neighbours):
    weight_vec, stiff_mat, deriv_mat, mass_two, lap_diag, upper_bound = tables
    lower_bound = upper_bound / bound_ratio
    midpoint = (upper_bound + lower_bound) / 2.0
    half_width = (upper_bound - lower_bound) / 2.0
    rhs = assemble(mass_two[None, None, :, :, None, None] * spectra, neighbours)
    diagonal = assemble(lap_diag[None, None, :, :, None, None] + coeff, neighbours)
    inverse = 1.0 / diagonal
    iterate = jnp.zeros_like(rhs)
    residual = rhs
    direction = inverse * residual / midpoint
    recurrence = half_width / midpoint
    for step in range(ITERS):
        iterate = iterate + direction
        residual = residual - assemble(helm_apply(direction, coeff, stiff_mat, weight_vec), neighbours)
        if step + 1 < ITERS:
            recurrence_next = 1.0 / (2.0 * midpoint / half_width - recurrence)
            direction = recurrence_next * recurrence * direction + 2.0 * recurrence_next / half_width * inverse * residual
            recurrence = recurrence_next
    return iterate

def reference(velocity, penalty):
    tables = gll_tables(ORDER)
    coeff = make_coeff(0, PLANES, penalty, tables[3])
    results = []
    for component in range(3):
        forcing = advect(velocity[0], velocity[1], velocity[component], tables[2])
        transformed = jnp.fft.rfft(forcing, axis=-1)[..., :MODES]
        spectra = jnp.concatenate([jnp.real(transformed), jnp.imag(transformed)], axis=-1) / math.sqrt(PLANES)
        spectra = jnp.moveaxis(spectra, -1, 0)[:, None].astype(jnp.float32)
        results.append(chebyshev(spectra, coeff, tables, no_neighbours))
    return jnp.concatenate(results, axis=1)
```

```python
import functools
import math

import jax
import jax.numpy as jnp
import ml_dtypes
import numpy as np
from jax import lax
from jax.experimental import pallas as pl
from jax.experimental.pallas import tpu as pltpu
from jax.sharding import PartitionSpec as P

ORDER = 10
NQ = ORDER + 1
NODES = NQ * NQ
PLANES = 512
MODES = 256
ITERS = 6
HELM_BASE = 1.0
SPAN_WAVE = 0.02
BOUND_RATIO = 25.0

COMPS = 3
PADDED = 128
OWNERS = 16
COLUMNS = 8
GROUPS = 2 * COMPS
HALF = ORDER // 2
MESH = pl.DeviceIdType.MESH
VMEM_LIMIT = 56 * 2**20


def legendre_pair(points, order):
    previous = points * 0.0 + 1.0
    current = points * 1.0
    for degree in range(2, order + 1):
        following = ((2 * degree - 1) * points * current - (degree - 1) * previous) / degree
        previous = current
        current = following
    return (current, previous)


def gll_tables(order):
    count = order + 1
    points = -np.cos(np.pi * np.arange(count) / order)
    for sweep in range(200):
        top_vals, below_vals = legendre_pair(points, order)
        points = points - (points * top_vals - below_vals) / (count * top_vals)
    legendre_vals, below_vals = legendre_pair(points, order)
    weights = 2.0 / (order * (order + 1) * legendre_vals**2)
    identity = np.eye(count)
    spacing = points[:, None] - points[None, :] + identity
    derivative = legendre_vals[:, None] / (legendre_vals[None, :] * spacing) * (1.0 - identity)
    corner = np.concatenate(
        [[-order * (order + 1) / 4.0], np.zeros(order - 1), [order * (order + 1) / 4.0]]
    )
    derivative = derivative + identity * corner[None, :]
    stiffness = derivative.T @ (weights[:, None] * derivative)
    weight_mat = identity * weights[None, :]
    laplace = np.kron(stiffness, weight_mat) + np.kron(weight_mat, stiffness)
    upper_bound = float(
        np.max(np.sum(np.abs(laplace), axis=1) / np.sum(laplace * np.eye(count * count), axis=1))
    )
    return weights, stiffness, derivative, upper_bound


WEIGHTS, STIFF, DERIV, TOP = gll_tables(ORDER)
SCALED = STIFF / WEIGHTS[:, None]


def chebyshev_table():
    low = TOP / BOUND_RATIO
    mid = (TOP + low) / 2.0
    half = (TOP - low) / 2.0
    table = [(0.0, 1.0 / mid)]
    recurrence = half / mid
    for step in range(ITERS - 1):
        following = 1.0 / (2.0 * mid / half - recurrence)
        table.append((following * recurrence, 2.0 * following / half))
        recurrence = following
    return np.asarray(table, np.float32).T.copy()


def dft_table():
    planes = np.arange(PLANES)
    modes = np.arange(MODES)
    angles = 2.0 * np.pi / PLANES * (modes[:, None] * planes[None, :] % PLANES)
    table = np.concatenate([np.cos(angles), -np.sin(angles)]) / math.sqrt(PLANES)
    high = table.astype(ml_dtypes.bfloat16)
    low = (table - high.astype(np.float64)).astype(ml_dtypes.bfloat16)
    return high, low


def lines(vals, matrix, sign):
    evens = [vals[k] + vals[ORDER - k] for k in range(HALF)]
    odds = [vals[k] - vals[ORDER - k] for k in range(HALF)]
    out = [None] * NQ
    for i in range(HALF):
        even = vals[HALF] * float(matrix[i, HALF])
        odd = None
        for k in range(HALF):
            even = even + evens[k] * float((matrix[i, k] + matrix[i, ORDER - k]) / 2)
            term = odds[k] * float((matrix[i, k] - matrix[i, ORDER - k]) / 2)
            odd = term if odd is None else odd + term
        out[i] = even + odd
        out[ORDER - i] = even - odd if sign > 0 else odd - even
    middle = vals[HALF] * float(matrix[HALF, HALF]) if sign > 0 else None
    for k in range(HALF):
        term = (evens if sign > 0 else odds)[k] * float(matrix[HALF, k])
        middle = term if middle is None else middle + term
    out[HALF] = middle
    return out


def roll(tile, by):
    return pltpu.roll(tile, by % 128, 1)


def forward_kernel(vel, high, low, out, tmp, forcing):
    forcing[pl.ds(NODES * 8, (PADDED - NODES) * 8), :] = jnp.zeros(
        ((PADDED - NODES) * 8, 128), jnp.float32
    )

    for c in range(COMPS):

        def first(b, _):
            grads = lines([vel[c * NODES + a * NQ + b] for a in range(NQ)], DERIV, -1)
            for a in range(NQ):
                tmp[a * NQ + b] = vel[a * NQ + b] * grads[a]
            return 0

        def second(a, _):
            vals = [vel[c * NODES + a * NQ + b] for b in range(NQ)]
            grads = lines(vals, DERIV, -1)
            for b in range(NQ):
                node = a * NQ + b
                value = vals[b] - (tmp[node] + vel[NODES + node] * grads[b])
                forcing[pl.ds(pl.multiple_of(node * 8, 8), 8), :] = value
            return 0

        lax.fori_loop(0, NQ, first, 0)
        lax.fori_loop(0, NQ, second, 0)
        for g in range(2):
            field = jnp.concatenate(
                [
                    jnp.concatenate(
                        [forcing[pl.ds(g * 512 + t * 2 + y, 64, stride=8), :] for y in range(2)],
                        axis=0,
                    )
                    for t in range(4)
                ],
                axis=1,
            )
            upper = field.astype(jnp.bfloat16)
            lower = (field - upper.astype(jnp.float32)).astype(jnp.bfloat16)
            dims = (((1,), (1,)), ((), ()))
            dot = functools.partial(
                lax.dot_general, dimension_numbers=dims, preferred_element_type=jnp.float32
            )
            spectra = dot(high[...], upper) + (dot(high[...], lower) + dot(low[...], upper))
            out[:, c * 2 + g] = spectra.reshape(OWNERS, 4, 8, 128)


def forward(velocity):
    tiles = velocity.reshape(COMPS * NODES, 2, 4, 128).transpose(0, 2, 1, 3)
    tiles = tiles.reshape(COMPS * NODES, 8, 128)
    high, low = dft_table()
    return pl.pallas_call(
        forward_kernel,
        out_shape=jax.ShapeDtypeStruct((OWNERS, GROUPS, 4, 8, 128), jnp.float32),
        scratch_shapes=[
            pltpu.VMEM((NODES, 8, 128), jnp.float32),
            pltpu.VMEM((PADDED * 8, 128), jnp.float32),
        ],
        compiler_params=pltpu.CompilerParams(vmem_limit_bytes=VMEM_LIMIT),
        name="forward",
    )(tiles, jnp.asarray(high), jnp.asarray(low))


def exchange_kernel(src, dst, send_sem, recv_sem, local_sem):
    me, column = lax.axis_index("mode"), lax.axis_index("mesh")
    barrier = pltpu.get_barrier_semaphore()
    for offset in range(1, OWNERS):
        pl.semaphore_signal(
            barrier,
            inc=1,
            device_id=(lax.rem(me + offset, OWNERS), column),
            device_id_type=MESH,
        )
    pl.semaphore_wait(barrier, OWNERS - 1)
    copies = []
    for offset in range(1, OWNERS):
        dest = lax.rem(me + offset, OWNERS)
        copy = pltpu.make_async_remote_copy(
            src_ref=src.at[dest],
            dst_ref=dst.at[me],
            send_sem=send_sem.at[offset],
            recv_sem=recv_sem.at[offset],
            device_id=(dest, column),
            device_id_type=MESH,
        )
        copy.start()
        copies.append(copy)
    local = pltpu.make_async_copy(src.at[me], dst.at[me], local_sem)
    local.start()
    local.wait()
    for copy in copies:
        copy.wait()


def exchange(spectra):
    return pl.pallas_call(
        exchange_kernel,
        out_shape=jax.ShapeDtypeStruct(spectra.shape, spectra.dtype),
        in_specs=[pl.BlockSpec(memory_space=pl.ANY)],
        out_specs=pl.BlockSpec(memory_space=pl.ANY),
        scratch_shapes=[
            pltpu.SemaphoreType.DMA((OWNERS,)),
            pltpu.SemaphoreType.DMA((OWNERS,)),
            pltpu.SemaphoreType.DMA,
        ],
        compiler_params=pltpu.CompilerParams(collective_id=0, has_side_effects=True),
        name="exchange",
    )(spectra)


def lane_bits():
    lane = lax.broadcasted_iota(jnp.int32, (8, 128), 1)
    return lane, lane // 64, lane // 16 % 4, lane % 16


def join_rows(low, high):
    _, parity, _, pair = lane_bits()
    above = jnp.where(parity == 0, roll(low, 64), roll(low, 63))
    below = jnp.where(parity == 1, roll(high, 64), roll(high, 65))
    last = (parity == 1) & (pair == 15)
    first = (parity == 0) & (pair == 0)
    return low + jnp.where(first, 0.0, below), high + jnp.where(last, 0.0, above)


def butterfly(tiles, first_bit):
    tiles = list(tiles)
    lane = lax.broadcasted_iota(jnp.int32, (8, 128), 1)
    for bit in range(3):
        width = 1 << (first_bit + bit)
        upper = lane // width % 2 == 1
        for i in range(8):
            if i >> bit & 1 == 0:
                j = i | 1 << bit
                a, b = tiles[i], tiles[j]
                tiles[i] = jnp.where(upper, roll(b, width), a)
                tiles[j] = jnp.where(upper, b, roll(a, -width))
    return tiles


def solve_kernel(
    spectra,
    penalty,
    laplace,
    table,
    out,
    res,
    direction,
    tmp,
    inverse,
    coeff,
    swap,
    sent,
    got,
    pen_sent,
    pen_got,
    send_sem,
    recv_sem,
    pen_send_sem,
    pen_recv_sem,
):
    mode, column = lax.axis_index("mode"), lax.axis_index("mesh")
    has = (column > 0, column < COLUMNS - 1)
    partner = (jnp.maximum(column - 1, 0), jnp.minimum(column + 1, COLUMNS - 1))
    edge_rows = (0, ORDER)

    def face_copy(step, c, side):
        return pltpu.make_async_remote_copy(
            src_ref=sent.at[step, c, side],
            dst_ref=got.at[step, c, 1 - side],
            send_sem=send_sem.at[step, c, side],
            recv_sem=recv_sem.at[step, c, 1 - side],
            device_id=(mode, partner[side]),
            device_id_type=MESH,
        )

    def pen_copy(side):
        return pltpu.make_async_remote_copy(
            src_ref=pen_sent.at[side],
            dst_ref=pen_got.at[1 - side],
            send_sem=pen_send_sem.at[side],
            recv_sem=pen_recv_sem.at[1 - side],
            device_id=(mode, partner[side]),
            device_id_type=MESH,
        )

    def start_faces(step, c):
        for side in range(2):

            @pl.when(has[side])
            def _():
                face_copy(step, c, side).start()

    def wait_faces(step, c):
        for side in range(2):

            @pl.when(has[side])
            def _():
                face_copy(step, c, side).wait_send()
                face_copy(step, c, 1 - side).wait_recv()

    for side in range(2):

        @pl.when(jnp.logical_not(has[side]))
        def _():
            for step in range(ITERS):
                got[step, :, side] = jnp.zeros((COMPS, NQ, 8, 128), jnp.float32)

    barrier = pltpu.get_barrier_semaphore()
    for side in range(2):

        @pl.when(has[side])
        def _():
            pl.semaphore_signal(
                barrier, inc=1, device_id=(mode, partner[side]), device_id_type=MESH
            )

    pl.semaphore_wait(barrier, has[0].astype(jnp.int32) + has[1].astype(jnp.int32))

    for side in range(2):
        pen_sent[side] = penalty[pl.ds(edge_rows[side] * NQ, 16), :]

        @pl.when(has[side])
        def _():
            pen_copy(side).start()

    def unpack(group, _):
        def low_bits(i, _):
            block, source = i // 2, (i % 2) * 8
            tiles = butterfly([spectra[source + k, group, block] for k in range(8)], 0)
            for k in range(8):
                swap[i * 8 + k] = tiles[k]
            return 0

        def high_bits(j, _):
            tiles = butterfly([swap[h * 8 + j] for h in range(8)], 3)
            for h in range(8):
                res[group * 64 + h * 8 + j] = tiles[h]
            return 0

        lax.fori_loop(0, 8, low_bits, 0)
        lax.fori_loop(0, 8, high_bits, 0)
        return 0

    lax.fori_loop(0, GROUPS, unpack, 0)

    for c in range(COMPS):

        def join_rhs(a, _):
            node = c * PADDED + a * NQ
            low, high = join_rows(res[node], res[node + ORDER])
            res[node] = low
            res[node + ORDER] = high
            return 0

        lax.fori_loop(0, NQ, join_rhs, 0)
        zero = jnp.zeros((8, 128), jnp.float32)
        for side in range(2):
            for b in range(NQ):
                node = c * PADDED + edge_rows[side] * NQ + b
                sent[0, c, side, b] = -res[node]
                res[node] = zero
                direction[node] = zero
                out[node] = zero
        start_faces(0, c)

    _, _, block, _ = lane_bits()
    row = mode * 32 + block * 8 + lax.broadcasted_iota(jnp.int32, (8, 128), 0)
    wave = (row % MODES).astype(jnp.float32)
    helm = HELM_BASE + (SPAN_WAVE * wave) * (SPAN_WAVE * wave)

    def make_coeff(node, _):
        value = helm + penalty[pl.ds(node, 1), :]
        coeff[node] = value
        inverse[node] = value + laplace[pl.ds(node, 1), :]
        return 0

    lax.fori_loop(0, NODES, make_coeff, 0)
    for side in range(2):

        @pl.when(has[side])
        def _():
            pen_copy(side).wait_send()
            pen_copy(1 - side).wait_recv()
            for b in range(NQ):
                node = edge_rows[side] * NQ + b
                other = helm + pen_got[side, pl.ds(b, 1), :]
                inverse[node] += other + laplace[pl.ds(node, 1), :]

    def invert(a, _):
        vals = [inverse[a * NQ + b] for b in range(NQ)]
        vals[0], vals[ORDER] = join_rows(vals[0], vals[ORDER])
        for b in range(NQ):
            inverse[a * NQ + b] = 1.0 / vals[b]
        return 0

    lax.fori_loop(0, NQ, invert, 0)

    for c in range(COMPS):

        def begin(i, _):
            node = NQ + i
            value = inverse[node] * res[c * PADDED + node] * table[1, 0]
            direction[c * PADDED + node] = value
            out[c * PADDED + node] = value
            return 0

        lax.fori_loop(0, NODES - 2 * NQ, begin, 0)

    def update(base, node, change, keep, gain):
        now = res[base + node] - change
        res[base + node] = now
        value = keep * direction[base + node] + gain * (inverse[node] * now)
        direction[base + node] = value
        out[base + node] += value

    def finish_faces(step, c):
        wait_faces(step, c)
        keep, gain = table[0, step], table[1, step]
        for side in range(2):
            for b in range(NQ):
                change = sent[step, c, side, b] + got[step, c, side, b]
                update(c * PADDED, edge_rows[side] * NQ + b, change, keep, gain)

    def along_second(base, a):
        terms = lines([direction[base + a * NQ + b] for b in range(NQ)], SCALED, 1)
        terms = [terms[b] + tmp[a * NQ + b] for b in range(NQ)]
        terms[0], terms[ORDER] = join_rows(terms[0], terms[ORDER])
        return terms

    def sweep(q, _):
        step, c = q // COMPS, q % COMPS
        base = c * PADDED
        finish_faces(step, c)

        def along_first(b, _):
            vals = [direction[base + a * NQ + b] for a in range(NQ)]
            terms = lines(vals, SCALED, 1)
            for a in range(NQ):
                tmp[a * NQ + b] = terms[a] + coeff[a * NQ + b] * vals[a]
            return 0

        lax.fori_loop(0, NQ, along_first, 0)
        for side in range(2):
            terms = along_second(base, edge_rows[side])
            for b in range(NQ):
                sent[step + 1, c, side, b] = terms[b]
        start_faces(step + 1, c)
        keep, gain = table[0, step + 1], table[1, step + 1]

        def interior(a, _):
            terms = along_second(base, a)
            for b in range(NQ):
                update(base, a * NQ + b, terms[b], keep, gain)
            return 0

        lax.fori_loop(1, ORDER, interior, 0)
        return 0

    lax.fori_loop(0, (ITERS - 1) * COMPS, sweep, 0)
    for c in range(COMPS):
        finish_faces(ITERS - 1, c)


def solve(spectra, penalty):
    pen = penalty.reshape(NODES, 16, 2).transpose(0, 2, 1)
    pen = jnp.broadcast_to(pen[:, :, None, :], (NODES, 2, 4, 16)).reshape(NODES, 128)
    pen = jnp.pad(pen, ((0, PADDED - NODES), (0, 0)))
    diag = np.diagonal(SCALED)
    laplace = np.zeros((PADDED, 128), np.float32)
    laplace[:NODES] = (diag[:, None] + diag[None, :]).reshape(NODES, 1)
    tile = (8, 128)
    vmem = pl.BlockSpec(memory_space=pltpu.VMEM)
    return pl.pallas_call(
        solve_kernel,
        out_shape=jax.ShapeDtypeStruct((COMPS * PADDED,) + tile, jnp.float32),
        in_specs=[vmem, vmem, vmem, pl.BlockSpec(memory_space=pltpu.SMEM)],
        out_specs=vmem,
        scratch_shapes=[
            pltpu.VMEM((COMPS * PADDED,) + tile, jnp.float32),
            pltpu.VMEM((COMPS * PADDED,) + tile, jnp.float32),
            pltpu.VMEM((PADDED,) + tile, jnp.float32),
            pltpu.VMEM((PADDED,) + tile, jnp.float32),
            pltpu.VMEM((PADDED,) + tile, jnp.float32),
            pltpu.VMEM((64,) + tile, jnp.float32),
            pltpu.VMEM((ITERS, COMPS, 2, NQ) + tile, jnp.float32),
            pltpu.VMEM((ITERS, COMPS, 2, NQ) + tile, jnp.float32),
            pltpu.VMEM((2, 16, 128), jnp.float32),
            pltpu.VMEM((2, 16, 128), jnp.float32),
            pltpu.SemaphoreType.DMA((ITERS, COMPS, 2)),
            pltpu.SemaphoreType.DMA((ITERS, COMPS, 2)),
            pltpu.SemaphoreType.DMA((2,)),
            pltpu.SemaphoreType.DMA((2,)),
        ],
        compiler_params=pltpu.CompilerParams(
            collective_id=1, has_side_effects=True, vmem_limit_bytes=VMEM_LIMIT
        ),
        name="solve",
    )(spectra, pen, jnp.asarray(laplace), jnp.asarray(chebyshev_table()))


def unpack_kernel(tiles, out):
    block = pl.program_id(0)
    lane = lax.broadcasted_iota(jnp.int32, (8, 128), 1)
    source = (lane % 2) * 64 + block * 16 + lane // 2 % 16
    for c in range(COMPS):

        def one(node, _):
            rows = jnp.take_along_axis(tiles[c * PADDED + node], source, axis=1)
            out[pl.ds(c * NODES + node, 8, stride=COMPS * NODES), :] = rows[:, :32]
            return 0

        lax.fori_loop(0, NODES, one, 0, unroll=11)


def unpack_output(tiles):
    rows = 8 * COMPS * NODES
    out = pl.pallas_call(
        unpack_kernel,
        grid=(4,),
        out_shape=jax.ShapeDtypeStruct((4 * rows, 32), jnp.float32),
        in_specs=[pl.BlockSpec(memory_space=pltpu.VMEM)],
        out_specs=pl.BlockSpec((rows, 32), lambda i: (i, 0)),
        compiler_params=pltpu.CompilerParams(vmem_limit_bytes=VMEM_LIMIT),
        name="unpack",
    )(tiles)
    return out.reshape(32, COMPS, NQ, NQ, 1, 32)


def per_device(velocity, penalty):
    return unpack_output(solve(exchange(forward(velocity)), penalty))


def solution(mesh):
    return jax.shard_map(
        per_device,
        mesh=mesh,
        in_specs=(P(None, None, None, "mesh", "mode", None), P(None, None, "mesh", None)),
        out_specs=P("mode", None, None, None, "mesh", None),
        check_vma=False,
    )
```

```python
import functools
import math

import jax
import jax.numpy as jnp
import ml_dtypes
import numpy as np
from jax import lax
from jax.experimental import pallas as pl
from jax.experimental.pallas import tpu as pltpu
from jax.sharding import PartitionSpec as P

ORDER = 10
NQ = ORDER + 1
NODES = NQ * NQ
PLANES = 512
MODES = 256
ITERS = 6
HELM_BASE = 1.0
SPAN_WAVE = 0.02
BOUND_RATIO = 25.0

COMPS = 3
PADDED = 128
OWNERS = 16
COLUMNS = 8
CHUNK = 64
HALF = ORDER // 2
UNROLL = True
MESH = pl.DeviceIdType.MESH
VMEM_LIMIT = 40 * 2**20


def legendre_pair(points, order):
    previous = points * 0.0 + 1.0
    current = points * 1.0
    for degree in range(2, order + 1):
        following = ((2 * degree - 1) * points * current - (degree - 1) * previous) / degree
        previous = current
        current = following
    return (current, previous)


def gll_tables(order):
    count = order + 1
    points = -np.cos(np.pi * np.arange(count) / order)
    for sweep in range(200):
        top_vals, below_vals = legendre_pair(points, order)
        points = points - (points * top_vals - below_vals) / (count * top_vals)
    legendre_vals, below_vals = legendre_pair(points, order)
    weights = 2.0 / (order * (order + 1) * legendre_vals**2)
    identity = np.eye(count)
    spacing = points[:, None] - points[None, :] + identity
    derivative = legendre_vals[:, None] / (legendre_vals[None, :] * spacing) * (1.0 - identity)
    corner = np.concatenate(
        [[-order * (order + 1) / 4.0], np.zeros(order - 1), [order * (order + 1) / 4.0]]
    )
    derivative = derivative + identity * corner[None, :]
    stiffness = derivative.T @ (weights[:, None] * derivative)
    weight_mat = identity * weights[None, :]
    laplace = np.kron(stiffness, weight_mat) + np.kron(weight_mat, stiffness)
    upper_bound = float(
        np.max(np.sum(np.abs(laplace), axis=1) / np.sum(laplace * np.eye(count * count), axis=1))
    )
    return weights, stiffness, derivative, upper_bound


WEIGHTS, STIFF, DERIV, TOP = gll_tables(ORDER)
SCALED = STIFF / WEIGHTS[:, None]


def chebyshev_table():
    low = TOP / BOUND_RATIO
    mid = (TOP + low) / 2.0
    half = (TOP - low) / 2.0
    table = [(0.0, 1.0 / mid)]
    recurrence = half / mid
    for step in range(ITERS - 1):
        following = 1.0 / (2.0 * mid / half - recurrence)
        table.append((following * recurrence, 2.0 * following / half))
        recurrence = following
    return np.asarray(table, np.float32).T.copy()


def dft_table():
    planes = np.arange(PLANES)
    modes = np.arange(MODES)
    angles = 2.0 * np.pi / PLANES * (modes[:, None] * planes[None, :] % PLANES)
    table = np.concatenate([np.cos(angles), -np.sin(angles)]) / math.sqrt(PLANES)
    high = table.astype(ml_dtypes.bfloat16)
    low = (table - high.astype(np.float64)).astype(ml_dtypes.bfloat16)
    return high, low


def lines(vals, matrix, sign):
    evens = [vals[k] + vals[ORDER - k] for k in range(HALF)]
    odds = [vals[k] - vals[ORDER - k] for k in range(HALF)]
    out = [None] * NQ
    for i in range(HALF):
        even = vals[HALF] * float(matrix[i, HALF])
        odd = None
        for k in range(HALF):
            even = even + evens[k] * float((matrix[i, k] + matrix[i, ORDER - k]) / 2)
            term = odds[k] * float((matrix[i, k] - matrix[i, ORDER - k]) / 2)
            odd = term if odd is None else odd + term
        out[i] = even + odd
        out[ORDER - i] = even - odd if sign > 0 else odd - even
    middle = vals[HALF] * float(matrix[HALF, HALF]) if sign > 0 else None
    for k in range(HALF):
        term = (evens if sign > 0 else odds)[k] * float(matrix[HALF, k])
        middle = term if middle is None else middle + term
    out[HALF] = middle
    return out


def roll(tile, by):
    return pltpu.roll(tile, by % 128, 1)


def join_rows(low, high):
    row = lax.broadcasted_iota(jnp.int32, (8, 128), 1) % 32
    above = jnp.where(row == 31, 0.0, roll(low, -1))
    below = jnp.where(row == 0, 0.0, roll(high, 1))
    return low + below, high + above


def step_kernel(
    vel,
    high,
    low,
    penalty,
    laplace,
    table,
    out,
    forcing,
    spectra,
    owned,
    res,
    direction,
    tmp,
    inverse,
    coeff,
    sent,
    got,
    pen_sent,
    pen_got,
    mode_send_sem,
    mode_recv_sem,
    local_sem,
    send_sem,
    recv_sem,
    pen_send_sem,
    pen_recv_sem,
):
    mode, column = lax.axis_index("mode"), lax.axis_index("mesh")
    has = (column > 0, column < COLUMNS - 1)
    partner = (jnp.maximum(column - 1, 0), jnp.minimum(column + 1, COLUMNS - 1))
    edge_rows = (0, ORDER)

    def chunk(c, owner):
        return pl.ds(pl.multiple_of((c * OWNERS + owner) * CHUNK, CHUNK), CHUNK)

    def mode_copy(c, offset):
        dest = lax.rem(mode + offset, OWNERS)
        return pltpu.make_async_remote_copy(
            src_ref=spectra.at[chunk(c, dest)],
            dst_ref=owned.at[chunk(c, mode)],
            send_sem=mode_send_sem.at[c, offset],
            recv_sem=mode_recv_sem.at[c, offset],
            device_id=(dest, column),
            device_id_type=MESH,
        )

    def local_copy(c):
        return pltpu.make_async_copy(
            spectra.at[chunk(c, mode)], owned.at[chunk(c, mode)], local_sem.at[c]
        )

    def face_copy(step, c, side):
        return pltpu.make_async_remote_copy(
            src_ref=sent.at[step, c, side],
            dst_ref=got.at[step, c, 1 - side],
            send_sem=send_sem.at[step, c, side],
            recv_sem=recv_sem.at[step, c, 1 - side],
            device_id=(mode, partner[side]),
            device_id_type=MESH,
        )

    def pen_copy(side):
        return pltpu.make_async_remote_copy(
            src_ref=pen_sent.at[side],
            dst_ref=pen_got.at[1 - side],
            send_sem=pen_send_sem.at[side],
            recv_sem=pen_recv_sem.at[1 - side],
            device_id=(mode, partner[side]),
            device_id_type=MESH,
        )

    def start_faces(step, c):
        for side in range(2):

            @pl.when(has[side])
            def _():
                face_copy(step, c, side).start()

    def wait_faces(step, c):
        for side in range(2):

            @pl.when(has[side])
            def _():
                face_copy(step, c, side).wait_send()
                face_copy(step, c, 1 - side).wait_recv()

    for side in range(2):

        @pl.when(jnp.logical_not(has[side]))
        def _():
            for step in range(ITERS):
                got[step, :, side] = jnp.zeros((COMPS, NQ, 8, 128), jnp.float32)

    barrier = pltpu.get_barrier_semaphore()
    for offset in range(1, OWNERS):
        dest = lax.rem(mode + offset, OWNERS)
        pl.semaphore_signal(barrier, inc=1, device_id=(dest, column), device_id_type=MESH)
    for side in range(2):

        @pl.when(has[side])
        def _():
            pl.semaphore_signal(
                barrier, inc=1, device_id=(mode, partner[side]), device_id_type=MESH
            )

    forcing[pl.ds(NODES * 8, (PADDED - NODES) * 8), :] = jnp.zeros(
        ((PADDED - NODES) * 8, 128), jnp.float32
    )
    for c in range(COMPS):

        def advect_first(b, _):
            grads = lines([vel[c * NODES + a * NQ + b] for a in range(NQ)], DERIV, -1)
            for a in range(NQ):
                tmp[a * NQ + b] = vel[a * NQ + b] * grads[a]
            return 0

        def advect_second(a, _):
            vals = [vel[c * NODES + a * NQ + b] for b in range(NQ)]
            grads = lines(vals, DERIV, -1)
            for b in range(NQ):
                node = a * NQ + b
                value = vals[b] - (tmp[node] + vel[NODES + node] * grads[b])
                forcing[pl.ds(pl.multiple_of(node * 8, 8), 8), :] = value
            return 0

        lax.fori_loop(0, NQ, advect_first, 0, unroll=UNROLL)
        lax.fori_loop(0, NQ, advect_second, 0, unroll=UNROLL)
        field = jnp.concatenate(
            [
                jnp.concatenate(
                    [forcing[pl.ds(t * 2 + y, PADDED, stride=8), :] for y in range(2)], axis=0
                )
                for t in range(4)
            ],
            axis=1,
        )
        upper = field.astype(jnp.bfloat16)
        lower = (field - upper.astype(jnp.float32)).astype(jnp.bfloat16)
        dot = functools.partial(
            lax.dot_general,
            dimension_numbers=(((1,), (1,)), ((), ())),
            preferred_element_type=jnp.float32,
        )
        modes = dot(high[...], upper) + (dot(high[...], lower) + dot(low[...], upper))
        for owner in range(OWNERS):
            for y in range(2):
                spectra[pl.ds((c * OWNERS + owner) * CHUNK + y * 32, 32), :] = modes[
                    owner * 32 : owner * 32 + 32, y * 128 : y * 128 + 128
                ]
        if c == 0:
            peers = OWNERS - 1 + has[0].astype(jnp.int32) + has[1].astype(jnp.int32)
            pl.semaphore_wait(barrier, peers)
        for offset in range(1, OWNERS):
            mode_copy(c, offset).start()
        local_copy(c).start()

    for side in range(2):
        pen_sent[side] = penalty[pl.ds(edge_rows[side] * NQ, 16), :]

        @pl.when(has[side])
        def _():
            pen_copy(side).start()

    block = lax.broadcasted_iota(jnp.int32, (8, 128), 1) // 32
    row = mode * 32 + block * 8 + lax.broadcasted_iota(jnp.int32, (8, 128), 0)
    wave = (row % MODES).astype(jnp.float32)
    helm = HELM_BASE + (SPAN_WAVE * wave) * (SPAN_WAVE * wave)

    def make_coeff(node, _):
        value = helm + penalty[pl.ds(node, 1), :]
        coeff[node] = value
        inverse[node] = value + laplace[pl.ds(node, 1), :]
        return 0

    lax.fori_loop(0, NODES, make_coeff, 0, unroll=11)
    for side in range(2):

        @pl.when(has[side])
        def _():
            pen_copy(side).wait_send()
            pen_copy(1 - side).wait_recv()
            for b in range(NQ):
                node = edge_rows[side] * NQ + b
                other = helm + pen_got[side, pl.ds(b, 1), :]
                inverse[node] += other + laplace[pl.ds(node, 1), :]

    def invert(a, _):
        vals = [inverse[a * NQ + b] for b in range(NQ)]
        vals[0], vals[ORDER] = join_rows(vals[0], vals[ORDER])
        for b in range(NQ):
            inverse[a * NQ + b] = 1.0 / vals[b]
        return 0

    lax.fori_loop(0, NQ, invert, 0, unroll=UNROLL)

    for c in range(COMPS):
        for offset in range(1, OWNERS):
            mode_copy(c, offset).wait_recv()
        local_copy(c).wait()

        def turn(r, _):
            first = c * OWNERS * CHUNK + r
            rows = [
                owned[pl.ds(first + (y * 32 + block * 8), 8, stride=32), :]
                for block in range(4)
                for y in range(0, 32, 8)
            ]
            tiles = jnp.concatenate(rows, axis=0).T
            for i in range(16):
                start = (c * PADDED + i * 8) * 8 + r
                res[pl.ds(start, 8, stride=8), :] = tiles[i * 8 : i * 8 + 8]
            return 0

        lax.fori_loop(0, 8, turn, 0, unroll=True)

        def join_rhs(a, _):
            node = c * PADDED + a * NQ
            low, high = join_rows(load(res, node), load(res, node + ORDER))
            store(res, node, low)
            store(res, node + ORDER, high)
            return 0

        lax.fori_loop(0, NQ, join_rhs, 0, unroll=UNROLL)
        zero = jnp.zeros((8, 128), jnp.float32)
        for side in range(2):
            for b in range(NQ):
                node = c * PADDED + edge_rows[side] * NQ + b
                sent[0, c, side, b] = -load(res, node)
                store(res, node, zero)
                direction[node] = zero
                out[node] = zero
        start_faces(0, c)

        def begin(i, _):
            node = NQ + i
            value = inverse[node] * load(res, c * PADDED + node) * table[1, 0]
            direction[c * PADDED + node] = value
            out[c * PADDED + node] = value
            return 0

        lax.fori_loop(0, NODES - 2 * NQ, begin, 0, unroll=11)

    def update(base, node, change, keep, gain):
        now = load(res, base + node) - change
        store(res, base + node, now)
        value = keep * direction[base + node] + gain * (inverse[node] * now)
        direction[base + node] = value
        out[base + node] += value

    def finish_faces(step, c):
        wait_faces(step, c)
        keep, gain = table[0, step], table[1, step]
        for side in range(2):
            for b in range(NQ):
                change = sent[step, c, side, b] + got[step, c, side, b]
                update(c * PADDED, edge_rows[side] * NQ + b, change, keep, gain)

    def along_second(base, a):
        terms = lines([direction[base + a * NQ + b] for b in range(NQ)], SCALED, 1)
        terms = [terms[b] + tmp[a * NQ + b] for b in range(NQ)]
        terms[0], terms[ORDER] = join_rows(terms[0], terms[ORDER])
        return terms

    def sweep(q, _):
        step, c = q // COMPS, q % COMPS
        base = c * PADDED
        finish_faces(step, c)

        def along_first(b, _):
            vals = [direction[base + a * NQ + b] for a in range(NQ)]
            terms = lines(vals, SCALED, 1)
            for a in range(NQ):
                tmp[a * NQ + b] = terms[a] + coeff[a * NQ + b] * vals[a]
            return 0

        lax.fori_loop(0, NQ, along_first, 0, unroll=UNROLL)
        for side in range(2):
            terms = along_second(base, edge_rows[side])
            for b in range(NQ):
                sent[step + 1, c, side, b] = terms[b]
        start_faces(step + 1, c)
        keep, gain = table[0, step + 1], table[1, step + 1]

        def interior(a, _):
            terms = along_second(base, a)
            for b in range(NQ):
                update(base, a * NQ + b, terms[b], keep, gain)
            return 0

        lax.fori_loop(1, ORDER, interior, 0, unroll=UNROLL)
        return 0

    lax.fori_loop(0, (ITERS - 1) * COMPS, sweep, 0)
    for c in range(COMPS):
        finish_faces(ITERS - 1, c)
        for offset in range(1, OWNERS):
            mode_copy(c, offset).wait_send()


def load(ref, node):
    return ref[pl.ds(pl.multiple_of(node * 8, 8), 8), :]


def store(ref, node, value):
    ref[pl.ds(pl.multiple_of(node * 8, 8), 8), :] = value


def run_step(velocity, penalty):
    tiles = velocity.reshape(COMPS * NODES, 2, 4, 128).transpose(0, 2, 1, 3)
    tiles = tiles.reshape(COMPS * NODES, 8, 128)
    high, low = dft_table()
    pen = jnp.tile(penalty.reshape(NODES, 32), (1, 4))
    pen = jnp.pad(pen, ((0, PADDED - NODES), (0, 0)))
    diag = np.diagonal(SCALED)
    laplace = np.zeros((PADDED, 128), np.float32)
    laplace[:NODES] = (diag[:, None] + diag[None, :]).reshape(NODES, 1)
    tile = (8, 128)
    vmem = pl.BlockSpec(memory_space=pltpu.VMEM)
    return pl.pallas_call(
        step_kernel,
        out_shape=jax.ShapeDtypeStruct((COMPS * PADDED,) + tile, jnp.float32),
        in_specs=[vmem] * 5 + [pl.BlockSpec(memory_space=pltpu.SMEM)],
        out_specs=vmem,
        scratch_shapes=[
            pltpu.VMEM((PADDED * 8, 128), jnp.float32),
            pltpu.VMEM((COMPS * OWNERS * CHUNK, 128), jnp.float32),
            pltpu.VMEM((COMPS * OWNERS * CHUNK, 128), jnp.float32),
            pltpu.VMEM((COMPS * PADDED * 8, 128), jnp.float32),
            pltpu.VMEM((COMPS * PADDED,) + tile, jnp.float32),
            pltpu.VMEM((PADDED,) + tile, jnp.float32),
            pltpu.VMEM((PADDED,) + tile, jnp.float32),
            pltpu.VMEM((PADDED,) + tile, jnp.float32),
            pltpu.VMEM((ITERS, COMPS, 2, NQ) + tile, jnp.float32),
            pltpu.VMEM((ITERS, COMPS, 2, NQ) + tile, jnp.float32),
            pltpu.VMEM((2, 16, 128), jnp.float32),
            pltpu.VMEM((2, 16, 128), jnp.float32),
            pltpu.SemaphoreType.DMA((COMPS, OWNERS)),
            pltpu.SemaphoreType.DMA((COMPS, OWNERS)),
            pltpu.SemaphoreType.DMA((COMPS,)),
            pltpu.SemaphoreType.DMA((ITERS, COMPS, 2)),
            pltpu.SemaphoreType.DMA((ITERS, COMPS, 2)),
            pltpu.SemaphoreType.DMA((2,)),
            pltpu.SemaphoreType.DMA((2,)),
        ],
        compiler_params=pltpu.CompilerParams(
            collective_id=0, has_side_effects=True, vmem_limit_bytes=VMEM_LIMIT
        ),
        name="step",
    )(tiles, jnp.asarray(high), jnp.asarray(low), pen, jnp.asarray(laplace), jnp.asarray(chebyshev_table()))


def unpack_kernel(tiles, out, rows, sem):
    size = 8 * COMPS * NODES
    copies = []
    for block in range(4):
        for c in range(COMPS):

            def one(node, _):
                tile = tiles[c * PADDED + node]
                if block:
                    tile = roll(tile, -32 * block)
                first = block * size + c * NODES + node
                rows[pl.ds(first, 8, stride=COMPS * NODES), :] = tile[:, :32]
                return 0

            lax.fori_loop(0, NODES, one, 0, unroll=11)
        part = pl.ds(block * size, size)
        copies.append(pltpu.make_async_copy(rows.at[part], out.at[part], sem.at[block]))
        copies[-1].start()
    for copy in copies:
        copy.wait()


def unpack_output(tiles):
    shape = (32 * COMPS * NODES, 32)
    out = pl.pallas_call(
        unpack_kernel,
        out_shape=jax.ShapeDtypeStruct(shape, jnp.float32),
        in_specs=[pl.BlockSpec(memory_space=pltpu.VMEM)],
        out_specs=pl.BlockSpec(memory_space=pl.ANY),
        scratch_shapes=[pltpu.VMEM(shape, jnp.float32), pltpu.SemaphoreType.DMA((4,))],
        compiler_params=pltpu.CompilerParams(vmem_limit_bytes=VMEM_LIMIT),
        name="unpack",
    )(tiles)
    return out.reshape(32, COMPS, NQ, NQ, 1, 32)


def per_device(velocity, penalty):
    return unpack_output(run_step(velocity, penalty))


def solution(mesh):
    return jax.shard_map(
        per_device,
        mesh=mesh,
        in_specs=(P(None, None, None, "mesh", "mode", None), P(None, None, "mesh", None)),
        out_specs=P("mode", None, None, None, "mesh", None),
        check_vma=False,
    )
```

```python
import functools
import math

import jax
import jax.numpy as jnp
import ml_dtypes
import numpy as np
from jax import lax
from jax.experimental import pallas as pl
from jax.experimental.pallas import tpu as pltpu
from jax.sharding import PartitionSpec as P

ORDER = 10
NQ = ORDER + 1
NODES = NQ * NQ
PLANES = 512
MODES = 256
ITERS = 6
HELM_BASE = 1.0
SPAN_WAVE = 0.02
BOUND_RATIO = 25.0

COMPS = 3
PADDED = 128
OWNERS = 16
COLUMNS = 8
CHUNK = 64
HALF = ORDER // 2
UNROLL = True
MESH = pl.DeviceIdType.MESH
VMEM_LIMIT = 60 * 2**20


def legendre_pair(points, order):
    previous = points * 0.0 + 1.0
    current = points * 1.0
    for degree in range(2, order + 1):
        following = ((2 * degree - 1) * points * current - (degree - 1) * previous) / degree
        previous = current
        current = following
    return (current, previous)


def gll_tables(order):
    count = order + 1
    points = -np.cos(np.pi * np.arange(count) / order)
    for sweep in range(200):
        top_vals, below_vals = legendre_pair(points, order)
        points = points - (points * top_vals - below_vals) / (count * top_vals)
    legendre_vals, below_vals = legendre_pair(points, order)
    weights = 2.0 / (order * (order + 1) * legendre_vals**2)
    identity = np.eye(count)
    spacing = points[:, None] - points[None, :] + identity
    derivative = legendre_vals[:, None] / (legendre_vals[None, :] * spacing) * (1.0 - identity)
    corner = np.concatenate(
        [[-order * (order + 1) / 4.0], np.zeros(order - 1), [order * (order + 1) / 4.0]]
    )
    derivative = derivative + identity * corner[None, :]
    stiffness = derivative.T @ (weights[:, None] * derivative)
    weight_mat = identity * weights[None, :]
    laplace = np.kron(stiffness, weight_mat) + np.kron(weight_mat, stiffness)
    upper_bound = float(
        np.max(np.sum(np.abs(laplace), axis=1) / np.sum(laplace * np.eye(count * count), axis=1))
    )
    return weights, stiffness, derivative, upper_bound


WEIGHTS, STIFF, DERIV, TOP = gll_tables(ORDER)
SCALED = STIFF / WEIGHTS[:, None]


def chebyshev_table():
    low = TOP / BOUND_RATIO
    mid = (TOP + low) / 2.0
    half = (TOP - low) / 2.0
    table = [(0.0, 1.0 / mid)]
    recurrence = half / mid
    for step in range(ITERS - 1):
        following = 1.0 / (2.0 * mid / half - recurrence)
        table.append((following * recurrence, 2.0 * following / half))
        recurrence = following
    return table


CHEBYSHEV = chebyshev_table()


def coefficients(step):
    keep, gain = CHEBYSHEV[0]
    for i in range(1, ITERS):
        keep = jnp.where(step == i, CHEBYSHEV[i][0], keep)
        gain = jnp.where(step == i, CHEBYSHEV[i][1], gain)
    return keep, gain


def dft_table():
    planes = np.arange(PLANES)
    modes = np.arange(MODES)
    angles = 2.0 * np.pi / PLANES * (modes[:, None] * planes[None, :] % PLANES)
    table = np.concatenate([np.cos(angles), -np.sin(angles)]) / math.sqrt(PLANES)
    high = table.astype(ml_dtypes.bfloat16)
    low = (table - high.astype(np.float64)).astype(ml_dtypes.bfloat16)
    return high, low


def lines(vals, matrix, sign):
    evens = [vals[k] + vals[ORDER - k] for k in range(HALF)]
    odds = [vals[k] - vals[ORDER - k] for k in range(HALF)]
    out = [None] * NQ
    for i in range(HALF):
        even = vals[HALF] * float(matrix[i, HALF])
        odd = None
        for k in range(HALF):
            even = even + evens[k] * float((matrix[i, k] + matrix[i, ORDER - k]) / 2)
            term = odds[k] * float((matrix[i, k] - matrix[i, ORDER - k]) / 2)
            odd = term if odd is None else odd + term
        out[i] = even + odd
        out[ORDER - i] = even - odd if sign > 0 else odd - even
    middle = vals[HALF] * float(matrix[HALF, HALF]) if sign > 0 else None
    for k in range(HALF):
        term = (evens if sign > 0 else odds)[k] * float(matrix[HALF, k])
        middle = term if middle is None else middle + term
    out[HALF] = middle
    return out


def edge_lines(vals):
    even = vals[HALF] * float(SCALED[0, HALF])
    odd = None
    for k in range(1, HALF):
        near, far = float(SCALED[0, k]), float(SCALED[0, ORDER - k])
        even = even + (vals[k] + vals[ORDER - k]) * ((near + far) / 2)
        term = (vals[k] - vals[ORDER - k]) * ((near - far) / 2)
        odd = term if odd is None else odd + term
    return even + odd, even - odd


def roll(tile, by):
    return pltpu.roll(tile, by % 128, 1)


def join_rows(low, high):
    row = lax.broadcasted_iota(jnp.int32, (8, 128), 1) % 32
    above = jnp.where(row == 31, 0.0, roll(low, -1))
    below = jnp.where(row == 0, 0.0, roll(high, 1))
    return low + below, high + above


def step_kernel(
    vel_in,
    high_in,
    low_in,
    pen_in,
    result,
    out,
    vel,
    high,
    low,
    pen_rows,
    penalty,
    edges,
    forcing,
    spectra,
    owned,
    res,
    direction,
    tmp,
    inverse,
    coeff,
    sent,
    got,
    pen_sent,
    pen_got,
    mode_send_sem,
    mode_recv_sem,
    local_sem,
    send_sem,
    recv_sem,
    pen_send_sem,
    pen_recv_sem,
    load_sem,
    out_sem,
):
    mode, column = lax.axis_index("mode"), lax.axis_index("mesh")
    has = (column > 0, column < COLUMNS - 1)
    partner = (jnp.maximum(column - 1, 0), jnp.minimum(column + 1, COLUMNS - 1))
    edge_rows = (0, ORDER)

    loads = [
        pltpu.make_async_copy(
            vel_in.at[pl.ds(c * NODES, NODES)], vel.at[pl.ds(c * NODES, NODES)], load_sem.at[c]
        )
        for c in range(COMPS)
    ]
    load_high = pltpu.make_async_copy(high_in, high, load_sem.at[3])
    load_low = pltpu.make_async_copy(low_in, low, load_sem.at[4])
    load_pen = pltpu.make_async_copy(pen_in, pen_rows, load_sem.at[5])
    for copy in [loads[0], loads[1], load_high, load_low, loads[2], load_pen]:
        copy.start()

    def chunk(c, owner):
        return pl.ds(pl.multiple_of((c * OWNERS + owner) * CHUNK, CHUNK), CHUNK)

    def mode_copy(c, offset):
        dest = lax.rem(mode + offset, OWNERS)
        return pltpu.make_async_remote_copy(
            src_ref=spectra.at[chunk(c, dest)],
            dst_ref=owned.at[chunk(c, mode)],
            send_sem=mode_send_sem.at[c, offset],
            recv_sem=mode_recv_sem.at[c, offset],
            device_id=(dest, column),
            device_id_type=MESH,
        )

    def local_copy(c):
        return pltpu.make_async_copy(
            spectra.at[chunk(c, mode)], owned.at[chunk(c, mode)], local_sem.at[c]
        )

    def face_copy(step, c, side):
        return pltpu.make_async_remote_copy(
            src_ref=sent.at[step, c, side],
            dst_ref=got.at[step, c, 1 - side],
            send_sem=send_sem.at[step, c, side],
            recv_sem=recv_sem.at[step, c, 1 - side],
            device_id=(mode, partner[side]),
            device_id_type=MESH,
        )

    def pen_copy(side):
        return pltpu.make_async_remote_copy(
            src_ref=pen_sent.at[side],
            dst_ref=pen_got.at[1 - side],
            send_sem=pen_send_sem.at[side],
            recv_sem=pen_recv_sem.at[1 - side],
            device_id=(mode, partner[side]),
            device_id_type=MESH,
        )

    def start_faces(step, c):
        for side in range(2):

            @pl.when(has[side])
            def _():
                face_copy(step, c, side).start()

    def wait_faces(step, c):
        for side in range(2):

            @pl.when(has[side])
            def _():
                face_copy(step, c, 1 - side).wait_recv()

    for side in range(2):

        @pl.when(jnp.logical_not(has[side]))
        def _():
            for step in range(ITERS):
                got[step, :, side] = jnp.zeros((COMPS, NQ, 8, 128), jnp.float32)

    barrier = pltpu.get_barrier_semaphore()
    for offset in range(1, OWNERS):
        dest = lax.rem(mode + offset, OWNERS)
        pl.semaphore_signal(barrier, inc=1, device_id=(dest, column), device_id_type=MESH)
    for side in range(2):

        @pl.when(has[side])
        def _():
            pl.semaphore_signal(
                barrier, inc=1, device_id=(mode, partner[side]), device_id_type=MESH
            )

    def node_rows(c, node):
        return pl.ds(pl.multiple_of((c * PADDED + node) * 8, 8), 8)

    def advect(c):
        pad = pl.ds((c * PADDED + NODES) * 8, (PADDED - NODES) * 8)
        forcing[pad, :] = jnp.zeros(((PADDED - NODES) * 8, 128), jnp.float32)

        def advect_first(b, _):
            grads = lines([vel[c * NODES + a * NQ + b] for a in range(NQ)], DERIV, -1)
            for a in range(NQ):
                tmp[a * NQ + b] = vel[a * NQ + b] * grads[a]
            return 0

        def advect_second(a, _):
            vals = [vel[c * NODES + a * NQ + b] for b in range(NQ)]
            grads = lines(vals, DERIV, -1)
            for b in range(NQ):
                node = a * NQ + b
                value = vals[b] - (tmp[node] + vel[NODES + node] * grads[b])
                forcing[node_rows(c, node), :] = value
            return 0

        lax.fori_loop(0, NQ, advect_first, 0, unroll=UNROLL)
        lax.fori_loop(0, NQ, advect_second, 0, unroll=UNROLL)

    def send_forcing_faces(c):
        for side in range(2):
            for b in range(NQ):
                sent[0, c, side, b] = forcing[node_rows(c, edge_rows[side] * NQ + b), :]
        start_faces(0, c)

    def add_forcing_faces(c):
        wait_faces(0, c)
        for side in range(2):
            for b in range(NQ):
                forcing[node_rows(c, edge_rows[side] * NQ + b), :] += got[0, c, side, b]

    def transform(c):
        field = jnp.concatenate(
            [
                jnp.concatenate(
                    [
                        forcing[pl.ds(c * PADDED * 8 + t * 2 + y, PADDED, stride=8), :]
                        for y in range(2)
                    ],
                    axis=0,
                )
                for t in range(4)
            ],
            axis=1,
        )
        upper = field.astype(jnp.bfloat16)
        lower = (field - upper.astype(jnp.float32)).astype(jnp.bfloat16)
        dot = functools.partial(
            lax.dot_general,
            dimension_numbers=(((1,), (1,)), ((), ())),
            preferred_element_type=jnp.float32,
        )
        modes = dot(high[...], upper) + (dot(high[...], lower) + dot(low[...], upper))
        for owner in range(OWNERS):
            for y in range(2):
                spectra[pl.ds((c * OWNERS + owner) * CHUNK + y * 32, 32), :] = modes[
                    owner * 32 : owner * 32 + 32, y * 128 : y * 128 + 128
                ]
        for offset in range(1, OWNERS):
            mode_copy(c, offset).start()
        local_copy(c).start()

    loads[0].wait()
    loads[1].wait()
    advect(0)
    advect(1)
    peers = OWNERS - 1 + has[0].astype(jnp.int32) + has[1].astype(jnp.int32)
    pl.semaphore_wait(barrier, peers)
    send_forcing_faces(1)
    load_high.wait()
    load_low.wait()
    transform(0)
    loads[2].wait()
    advect(2)
    send_forcing_faces(2)

    load_pen.wait()
    for node in range(NODES):
        line = pen_rows[node]
        penalty[pl.ds(node, 1), :] = jnp.concatenate([line] * 4, axis=1)
    for side in range(2):
        for b in range(NQ):
            node = edge_rows[side] * NQ + b
            pen_sent[side, pl.ds(b, 1), :] = penalty[pl.ds(node, 1), :]
        pen_sent[side, pl.ds(NQ, 16 - NQ), :] = jnp.zeros((16 - NQ, 128), jnp.float32)

        @pl.when(has[side])
        def _():
            pen_copy(side).start()

    add_forcing_faces(1)
    transform(1)

    block = lax.broadcasted_iota(jnp.int32, (8, 128), 1) // 32
    row = mode * 32 + block * 8 + lax.broadcasted_iota(jnp.int32, (8, 128), 0)
    wave = (row % MODES).astype(jnp.float32)
    helm = HELM_BASE + (SPAN_WAVE * wave) * (SPAN_WAVE * wave)

    diag = [float(SCALED[i, i]) for i in range(NQ)]
    for a in range(NQ):
        for b in range(NQ):
            value = helm + penalty[pl.ds(a * NQ + b, 1), :]
            coeff[a * NQ + b] = value
            inverse[a * NQ + b] = value + (diag[a] + diag[b])

    add_forcing_faces(2)
    transform(2)

    for side in range(2):

        @pl.when(has[side])
        def _():
            pen_copy(1 - side).wait_recv()
            for b in range(NQ):
                node = edge_rows[side] * NQ + b
                other = helm + pen_got[side, pl.ds(b, 1), :]
                inverse[node] += other + (diag[edge_rows[side]] + diag[b])

    for a in range(NQ):
        vals = [inverse[a * NQ + b] for b in range(NQ)]
        vals[0], vals[ORDER] = join_rows(vals[0], vals[ORDER])
        for b in range(NQ):
            inverse[a * NQ + b] = 1.0 / vals[b]

    def begin(c):
        for offset in range(1, OWNERS):
            mode_copy(c, offset).wait_recv()
        local_copy(c).wait()
        for r in range(8):
            first = c * OWNERS * CHUNK + r
            rows = [
                owned[pl.ds(first + (y * 32 + block * 8), 8, stride=32), :]
                for block in range(4)
                for y in range(0, 32, 8)
            ]
            tiles = jnp.concatenate(rows, axis=0).T
            for i in range(16):
                start = (c * PADDED + i * 8) * 8 + r
                res[pl.ds(start, 8, stride=8), :] = tiles[i * 8 : i * 8 + 8]
        for a in range(NQ):
            node = c * PADDED + a * NQ
            low, high = join_rows(load(res, node), load(res, node + ORDER))
            store(res, node, low)
            store(res, node + ORDER, high)
        nodes = range(NODES)
        if c == 0:
            zero = jnp.zeros((8, 128), jnp.float32)
            for side in range(2):
                for b in range(NQ):
                    node = edge_rows[side] * NQ + b
                    sent[0, c, side, b] = -load(res, node)
                    store(res, node, zero)
                    direction[node] = zero
                    out[node] = zero
            start_faces(0, c)
            nodes = range(NQ, NODES - NQ)
        for i in nodes:
            value = inverse[i] * load(res, c * PADDED + i) * CHEBYSHEV[0][1]
            direction[c * PADDED + i] = value
            out[c * PADDED + i] = value
        prepare_edges(c)

    def update(base, node, change, keep, gain):
        now = load(res, base + node) - change
        store(res, base + node, now)
        value = keep * direction[base + node] + gain * (inverse[node] * now)
        direction[base + node] = value
        out[base + node] += value

    def finish_faces(step, c):
        wait_faces(step, c)
        keep, gain = coefficients(step)
        for side in range(2):
            for b in range(NQ):
                change = sent[step, c, side, b] + got[step, c, side, b]
                update(c * PADDED, edge_rows[side] * NQ + b, change, keep, gain)

    def prepare_edges(c):
        for b in range(NQ):
            vals = [direction[c * PADDED + a * NQ + b] for a in range(1, ORDER)]
            edges[c * 2 * NQ + b], edges[c * 2 * NQ + NQ + b] = edge_lines([None] + vals + [None])

    def send_edges(step, c):
        base = c * PADDED
        own, across = float(SCALED[0, 0]), float(SCALED[0, ORDER])
        for side in range(2):
            node = edge_rows[side] * NQ
            other = edge_rows[1 - side] * NQ
            vals = [direction[base + node + b] for b in range(NQ)]
            terms = lines(vals, SCALED, 1)
            for b in range(NQ):
                first = edges[c * 2 * NQ + side * NQ + b] + direction[base + other + b] * across
                terms[b] = terms[b] + first + vals[b] * (coeff[node + b] + own)
            terms[0], terms[ORDER] = join_rows(terms[0], terms[ORDER])
            for b in range(NQ):
                sent[step, c, side, b] = terms[b]
        start_faces(step, c)

    def interior(step, c):
        base = c * PADDED
        keep, gain = coefficients(step)

        def along_first(b, _):
            vals = [direction[base + a * NQ + b] for a in range(NQ)]
            terms = lines(vals, SCALED, 1)
            for a in range(1, ORDER):
                tmp[a * NQ + b] = terms[a] + coeff[a * NQ + b] * vals[a]
            return 0

        def along_second(a, _):
            terms = lines([direction[base + a * NQ + b] for b in range(NQ)], SCALED, 1)
            terms = [terms[b] + tmp[a * NQ + b] for b in range(NQ)]
            terms[0], terms[ORDER] = join_rows(terms[0], terms[ORDER])
            for b in range(NQ):
                update(base, a * NQ + b, terms[b], keep, gain)
            return 0

        lax.fori_loop(0, NQ, along_first, 0, unroll=UNROLL)
        lax.fori_loop(1, ORDER, along_second, 0, unroll=UNROLL)
        prepare_edges(c)

    def sweep(q, _):
        step, c = q // COMPS, q % COMPS
        finish_faces(step, c)
        send_edges(step + 1, c)
        interior(step + 1, c)
        return 0

    begin(0)
    finish_faces(0, 0)
    for c in range(COMPS):
        send_edges(1, c)
        interior(1, c)
        if c + 1 < COMPS:
            begin(c + 1)
    lax.fori_loop(COMPS, (ITERS - 1) * COMPS, sweep, 0)
    saves = []
    for c in range(COMPS):
        finish_faces(ITERS - 1, c)
        part = pl.ds(c * PADDED, NODES)
        saves.append(pltpu.make_async_copy(out.at[part], result.at[part], out_sem.at[c]))
        saves[-1].start()

    for c in range(COMPS):
        saves[c].wait()
        for offset in range(1, OWNERS):
            mode_copy(c, offset).wait_send()
    for side in range(2):

        @pl.when(has[side])
        def _():
            pen_copy(side).wait_send()
            for step in range(ITERS):
                for c in range(COMPS):
                    face_copy(step, c, side).wait_send()


def load(ref, node):
    return ref[pl.ds(pl.multiple_of(node * 8, 8), 8), :]


def store(ref, node, value):
    ref[pl.ds(pl.multiple_of(node * 8, 8), 8), :] = value


def run_step(velocity, penalty):
    tiles = velocity.reshape(COMPS * NODES, 2, 4, 128).transpose(0, 2, 1, 3)
    tiles = tiles.reshape(COMPS * NODES, 8, 128)
    high, low = dft_table()
    pen = penalty.reshape(NODES, 1, 32)
    tile = (8, 128)
    return pl.pallas_call(
        step_kernel,
        out_shape=jax.ShapeDtypeStruct((COMPS * PADDED,) + tile, jnp.float32),
        in_specs=[pl.BlockSpec(memory_space=pltpu.HBM)] * 4,
        out_specs=pl.BlockSpec(memory_space=pltpu.HBM),
        scratch_shapes=[
            pltpu.VMEM((COMPS * PADDED,) + tile, jnp.float32),
            pltpu.VMEM((COMPS * NODES,) + tile, jnp.float32),
            pltpu.VMEM((PLANES, PLANES), jnp.bfloat16),
            pltpu.VMEM((PLANES, PLANES), jnp.bfloat16),
            pltpu.VMEM((NODES, 1, 32), jnp.float32),
            pltpu.VMEM((PADDED, 128), jnp.float32),
            pltpu.VMEM((COMPS * 2 * NQ,) + tile, jnp.float32),
            pltpu.VMEM((COMPS * PADDED * 8, 128), jnp.float32),
            pltpu.VMEM((COMPS * OWNERS * CHUNK, 128), jnp.float32),
            pltpu.VMEM((COMPS * OWNERS * CHUNK, 128), jnp.float32),
            pltpu.VMEM((COMPS * PADDED * 8, 128), jnp.float32),
            pltpu.VMEM((COMPS * PADDED,) + tile, jnp.float32),
            pltpu.VMEM((PADDED,) + tile, jnp.float32),
            pltpu.VMEM((PADDED,) + tile, jnp.float32),
            pltpu.VMEM((PADDED,) + tile, jnp.float32),
            pltpu.VMEM((ITERS, COMPS, 2, NQ) + tile, jnp.float32),
            pltpu.VMEM((ITERS, COMPS, 2, NQ) + tile, jnp.float32),
            pltpu.VMEM((2, 16, 128), jnp.float32),
            pltpu.VMEM((2, 16, 128), jnp.float32),
            pltpu.SemaphoreType.DMA((COMPS, OWNERS)),
            pltpu.SemaphoreType.DMA((COMPS, OWNERS)),
            pltpu.SemaphoreType.DMA((COMPS,)),
            pltpu.SemaphoreType.DMA((ITERS, COMPS, 2)),
            pltpu.SemaphoreType.DMA((ITERS, COMPS, 2)),
            pltpu.SemaphoreType.DMA((2,)),
            pltpu.SemaphoreType.DMA((2,)),
            pltpu.SemaphoreType.DMA((6,)),
            pltpu.SemaphoreType.DMA((COMPS,)),
        ],
        compiler_params=pltpu.CompilerParams(
            collective_id=0, has_side_effects=True, vmem_limit_bytes=VMEM_LIMIT
        ),
        name="step",
    )(tiles, jnp.asarray(high), jnp.asarray(low), pen)


def unpack_kernel(tiles_in, out, tiles, rows, load_sem, sem):
    loads = []
    for c in range(COMPS):
        part = pl.ds(c * PADDED, NODES)
        loads.append(pltpu.make_async_copy(tiles_in.at[part], tiles.at[part], load_sem.at[c]))
        loads[-1].start()
    size = 8 * COMPS * NODES
    copies = []
    for block in range(4):
        for c in range(COMPS):
            if block == 0:
                loads[c].wait()
            for node in range(NODES):
                tile = tiles[c * PADDED + node]
                if block:
                    tile = roll(tile, -32 * block)
                first = block * size + c * NODES + node
                rows[pl.ds(first, 8, stride=COMPS * NODES), :] = tile[:, :32]
        part = pl.ds(block * size, size)
        copies.append(pltpu.make_async_copy(rows.at[part], out.at[part], sem.at[block]))
        copies[-1].start()
    for copy in copies:
        copy.wait()


def unpack_output(tiles):
    shape = (32 * COMPS * NODES, 32)
    out = pl.pallas_call(
        unpack_kernel,
        out_shape=jax.ShapeDtypeStruct(shape, jnp.float32),
        in_specs=[pl.BlockSpec(memory_space=pltpu.HBM)],
        out_specs=pl.BlockSpec(memory_space=pltpu.HBM),
        scratch_shapes=[
            pltpu.VMEM(tiles.shape, jnp.float32),
            pltpu.VMEM(shape, jnp.float32),
            pltpu.SemaphoreType.DMA((COMPS,)),
            pltpu.SemaphoreType.DMA((4,)),
        ],
        compiler_params=pltpu.CompilerParams(vmem_limit_bytes=VMEM_LIMIT),
        name="unpack",
    )(tiles)
    return out.reshape(32, COMPS, NQ, NQ, 1, 32)


def per_device(velocity, penalty):
    return unpack_output(run_step(velocity, penalty))


def solution(mesh):
    return jax.shard_map(
        per_device,
        mesh=mesh,
        in_specs=(P(None, None, None, "mesh", "mode", None), P(None, None, "mesh", None)),
        out_specs=P("mode", None, None, None, "mesh", None),
        check_vma=False,
    )
```

```python
import functools
import math

import jax
import jax.numpy as jnp
import ml_dtypes
import numpy as np
from jax import lax
from jax.experimental import pallas as pl
from jax.experimental.pallas import tpu as pltpu
from jax.sharding import PartitionSpec as P

ORDER = 10
NQ = ORDER + 1
NODES = NQ * NQ
PLANES = 512
MODES = 256
ITERS = 6
HELM_BASE = 1.0
SPAN_WAVE = 0.02
BOUND_RATIO = 25.0

COMPS = 3
PADDED = 128
OWNERS = 16
COLUMNS = 8
CHUNK = 64
HALF = ORDER // 2
UNROLL = True
MESH = pl.DeviceIdType.MESH
VMEM_LIMIT = 60 * 2**20


def legendre_pair(points, order):
    previous = points * 0.0 + 1.0
    current = points * 1.0
    for degree in range(2, order + 1):
        following = ((2 * degree - 1) * points * current - (degree - 1) * previous) / degree
        previous = current
        current = following
    return (current, previous)


def gll_tables(order):
    count = order + 1
    points = -np.cos(np.pi * np.arange(count) / order)
    for sweep in range(200):
        top_vals, below_vals = legendre_pair(points, order)
        points = points - (points * top_vals - below_vals) / (count * top_vals)
    legendre_vals, below_vals = legendre_pair(points, order)
    weights = 2.0 / (order * (order + 1) * legendre_vals**2)
    identity = np.eye(count)
    spacing = points[:, None] - points[None, :] + identity
    derivative = legendre_vals[:, None] / (legendre_vals[None, :] * spacing) * (1.0 - identity)
    corner = np.concatenate(
        [[-order * (order + 1) / 4.0], np.zeros(order - 1), [order * (order + 1) / 4.0]]
    )
    derivative = derivative + identity * corner[None, :]
    stiffness = derivative.T @ (weights[:, None] * derivative)
    weight_mat = identity * weights[None, :]
    laplace = np.kron(stiffness, weight_mat) + np.kron(weight_mat, stiffness)
    upper_bound = float(
        np.max(np.sum(np.abs(laplace), axis=1) / np.sum(laplace * np.eye(count * count), axis=1))
    )
    return weights, stiffness, derivative, upper_bound


WEIGHTS, STIFF, DERIV, TOP = gll_tables(ORDER)
SCALED = STIFF / WEIGHTS[:, None]


def chebyshev_table():
    low = TOP / BOUND_RATIO
    mid = (TOP + low) / 2.0
    half = (TOP - low) / 2.0
    table = [(0.0, 1.0 / mid)]
    recurrence = half / mid
    for step in range(ITERS - 1):
        following = 1.0 / (2.0 * mid / half - recurrence)
        table.append((following * recurrence, 2.0 * following / half))
        recurrence = following
    return table


CHEBYSHEV = chebyshev_table()


def coefficients(step):
    keep, gain = CHEBYSHEV[0]
    for i in range(1, ITERS):
        keep = jnp.where(step == i, CHEBYSHEV[i][0], keep)
        gain = jnp.where(step == i, CHEBYSHEV[i][1], gain)
    return keep, gain


def dft_table():
    planes = np.arange(PLANES)
    modes = np.arange(MODES)
    angles = 2.0 * np.pi / PLANES * (modes[:, None] * planes[None, :] % PLANES)
    table = np.concatenate([np.cos(angles), -np.sin(angles)]) / math.sqrt(PLANES)
    high = table.astype(ml_dtypes.bfloat16)
    low = (table - high.astype(np.float64)).astype(ml_dtypes.bfloat16)
    return high, low


def lines(vals, matrix, sign):
    evens = [vals[k] + vals[ORDER - k] for k in range(HALF)]
    odds = [vals[k] - vals[ORDER - k] for k in range(HALF)]
    out = [None] * NQ
    for i in range(HALF):
        even = vals[HALF] * float(matrix[i, HALF])
        odd = None
        for k in range(HALF):
            even = even + evens[k] * float((matrix[i, k] + matrix[i, ORDER - k]) / 2)
            term = odds[k] * float((matrix[i, k] - matrix[i, ORDER - k]) / 2)
            odd = term if odd is None else odd + term
        out[i] = even + odd
        out[ORDER - i] = even - odd if sign > 0 else odd - even
    middle = vals[HALF] * float(matrix[HALF, HALF]) if sign > 0 else None
    for k in range(HALF):
        term = (evens if sign > 0 else odds)[k] * float(matrix[HALF, k])
        middle = term if middle is None else middle + term
    out[HALF] = middle
    return out


def edge_lines(vals):
    even = vals[HALF] * float(SCALED[0, HALF])
    odd = None
    for k in range(1, HALF):
        near, far = float(SCALED[0, k]), float(SCALED[0, ORDER - k])
        even = even + (vals[k] + vals[ORDER - k]) * ((near + far) / 2)
        term = (vals[k] - vals[ORDER - k]) * ((near - far) / 2)
        odd = term if odd is None else odd + term
    return even + odd, even - odd


def roll(tile, by):
    return pltpu.roll(tile, by % 128, 1)


def join_rows(low, high):
    row = lax.broadcasted_iota(jnp.int32, (8, 128), 1) % 32
    above = jnp.where(row == 31, 0.0, roll(low, -1))
    below = jnp.where(row == 0, 0.0, roll(high, 1))
    return low + below, high + above


def step_kernel(
    vel_in,
    high_in,
    low_in,
    pen_in,
    result,
    out,
    vel,
    high,
    low,
    pen_rows,
    penalty,
    edges,
    faces,
    forcing,
    spectra,
    owned,
    res,
    direction,
    tmp,
    inverse,
    coeff,
    sent,
    got,
    pen_sent,
    pen_got,
    mode_send_sem,
    mode_recv_sem,
    local_sem,
    send_sem,
    recv_sem,
    pen_send_sem,
    pen_recv_sem,
    load_sem,
    out_sem,
):
    mode, column = lax.axis_index("mode"), lax.axis_index("mesh")

    def neighbour(side):
        return column + 2 * side - 1

    def has_neighbour(side):
        return (neighbour(side) >= 0) & (neighbour(side) < COLUMNS)

    has = (has_neighbour(0), has_neighbour(1))
    partner = (jnp.maximum(column - 1, 0), jnp.minimum(column + 1, COLUMNS - 1))
    inner = jnp.where(column < COLUMNS // 2, 1, 0)
    outer = 1 - inner
    edge_rows = (0, ORDER)

    loads = [
        pltpu.make_async_copy(
            vel_in.at[pl.ds(c * NODES, NODES)], vel.at[pl.ds(c * NODES, NODES)], load_sem.at[c]
        )
        for c in range(COMPS)
    ]
    load_high = pltpu.make_async_copy(high_in, high, load_sem.at[3])
    load_low = pltpu.make_async_copy(low_in, low, load_sem.at[4])
    load_pen = pltpu.make_async_copy(pen_in, pen_rows, load_sem.at[5])
    for copy in [loads[0], loads[1], load_high, load_low, loads[2], load_pen]:
        copy.start()

    def chunk(c, owner):
        return pl.ds(pl.multiple_of((c * OWNERS + owner) * CHUNK, CHUNK), CHUNK)

    def mode_copy(c, offset):
        dest = lax.rem(mode + offset, OWNERS)
        return pltpu.make_async_remote_copy(
            src_ref=spectra.at[chunk(c, dest)],
            dst_ref=owned.at[chunk(c, mode)],
            send_sem=mode_send_sem.at[c, offset],
            recv_sem=mode_recv_sem.at[c, offset],
            device_id=(dest, column),
            device_id_type=MESH,
        )

    def local_copy(c):
        return pltpu.make_async_copy(
            spectra.at[chunk(c, mode)], owned.at[chunk(c, mode)], local_sem.at[c]
        )

    def face_copy(step, c, side):
        return pltpu.make_async_remote_copy(
            src_ref=sent.at[step, c, side],
            dst_ref=got.at[step, c, 1 - side],
            send_sem=send_sem.at[step, c, side],
            recv_sem=recv_sem.at[step, c, 1 - side],
            device_id=(mode, jnp.clip(neighbour(side), 0, COLUMNS - 1)),
            device_id_type=MESH,
        )

    def pen_copy(side):
        return pltpu.make_async_remote_copy(
            src_ref=pen_sent.at[side],
            dst_ref=pen_got.at[1 - side],
            send_sem=pen_send_sem.at[side],
            recv_sem=pen_recv_sem.at[1 - side],
            device_id=(mode, partner[side]),
            device_id_type=MESH,
        )

    def start_face(step, c, side):
        @pl.when(has_neighbour(side))
        def _():
            face_copy(step, c, side).start()

    def wait_face(step, c, side):
        @pl.when(has_neighbour(side))
        def _():
            face_copy(step, c, 1 - side).wait_recv()

    def start_faces(step, c):
        for side in range(2):
            start_face(step, c, side)

    def wait_faces(step, c):
        for side in range(2):
            wait_face(step, c, side)

    for side in range(2):

        @pl.when(jnp.logical_not(has[side]))
        def _():
            for step in range(ITERS):
                got[step, :, side] = jnp.zeros((COMPS, NQ, 8, 128), jnp.float32)

    barrier = pltpu.get_barrier_semaphore()
    for offset in range(1, OWNERS):
        dest = lax.rem(mode + offset, OWNERS)
        pl.semaphore_signal(barrier, inc=1, device_id=(dest, column), device_id_type=MESH)
    for side in range(2):

        @pl.when(has[side])
        def _():
            pl.semaphore_signal(
                barrier, inc=1, device_id=(mode, partner[side]), device_id_type=MESH
            )

    def node_rows(c, node):
        return pl.ds(pl.multiple_of((c * PADDED + node) * 8, 8), 8)

    def advect(c):
        pad = pl.ds((c * PADDED + NODES) * 8, (PADDED - NODES) * 8)
        forcing[pad, :] = jnp.zeros(((PADDED - NODES) * 8, 128), jnp.float32)

        def advect_first(b, _):
            grads = lines([vel[c * NODES + a * NQ + b] for a in range(NQ)], DERIV, -1)
            for a in range(NQ):
                tmp[a * NQ + b] = vel[a * NQ + b] * grads[a]
            return 0

        def advect_second(a, _):
            vals = [vel[c * NODES + a * NQ + b] for b in range(NQ)]
            grads = lines(vals, DERIV, -1)
            for b in range(NQ):
                node = a * NQ + b
                value = vals[b] - (tmp[node] + vel[NODES + node] * grads[b])
                forcing[node_rows(c, node), :] = value
            return 0

        lax.fori_loop(0, NQ, advect_first, 0, unroll=UNROLL)
        lax.fori_loop(0, NQ, advect_second, 0, unroll=UNROLL)

    def send_forcing_faces(c):
        for side in range(2):
            for b in range(NQ):
                sent[0, c, side, b] = forcing[node_rows(c, edge_rows[side] * NQ + b), :]
        start_faces(0, c)

    def add_forcing_faces(c):
        wait_faces(0, c)
        for side in range(2):
            for b in range(NQ):
                forcing[node_rows(c, edge_rows[side] * NQ + b), :] += got[0, c, side, b]

    def transform(c):
        field = jnp.concatenate(
            [
                jnp.concatenate(
                    [
                        forcing[pl.ds(c * PADDED * 8 + t * 2 + y, PADDED, stride=8), :]
                        for y in range(2)
                    ],
                    axis=0,
                )
                for t in range(4)
            ],
            axis=1,
        )
        upper = field.astype(jnp.bfloat16)
        lower = (field - upper.astype(jnp.float32)).astype(jnp.bfloat16)
        dot = functools.partial(
            lax.dot_general,
            dimension_numbers=(((1,), (1,)), ((), ())),
            preferred_element_type=jnp.float32,
        )
        modes = dot(high[...], upper) + (dot(high[...], lower) + dot(low[...], upper))
        for owner in range(OWNERS):
            for y in range(2):
                spectra[pl.ds((c * OWNERS + owner) * CHUNK + y * 32, 32), :] = modes[
                    owner * 32 : owner * 32 + 32, y * 128 : y * 128 + 128
                ]
        for offset in range(1, OWNERS):
            mode_copy(c, offset).start()
        local_copy(c).start()

    loads[0].wait()
    loads[1].wait()
    advect(0)
    advect(1)
    peers = OWNERS - 1 + has[0].astype(jnp.int32) + has[1].astype(jnp.int32)
    pl.semaphore_wait(barrier, peers)
    send_forcing_faces(1)
    load_high.wait()
    load_low.wait()
    transform(0)
    loads[2].wait()
    advect(2)
    send_forcing_faces(2)

    load_pen.wait()
    for node in range(NODES):
        line = pen_rows[node]
        penalty[pl.ds(node, 1), :] = jnp.concatenate([line] * 4, axis=1)
    for side in range(2):
        for b in range(NQ):
            node = edge_rows[side] * NQ + b
            pen_sent[side, pl.ds(b, 1), :] = penalty[pl.ds(node, 1), :]
        pen_sent[side, pl.ds(NQ, 16 - NQ), :] = jnp.zeros((16 - NQ, 128), jnp.float32)

        @pl.when(has[side])
        def _():
            pen_copy(side).start()

    add_forcing_faces(1)
    transform(1)

    block = lax.broadcasted_iota(jnp.int32, (8, 128), 1) // 32
    row = mode * 32 + block * 8 + lax.broadcasted_iota(jnp.int32, (8, 128), 0)
    wave = (row % MODES).astype(jnp.float32)
    helm = HELM_BASE + (SPAN_WAVE * wave) * (SPAN_WAVE * wave)

    diag = [float(SCALED[i, i]) for i in range(NQ)]
    for a in range(NQ):
        for b in range(NQ):
            value = helm + penalty[pl.ds(a * NQ + b, 1), :]
            coeff[a * NQ + b] = value
            inverse[a * NQ + b] = value + (diag[a] + diag[b])

    add_forcing_faces(2)
    transform(2)

    for side in range(2):
        for b in range(NQ):
            faces[side * NQ + b] = coeff[edge_rows[side] * NQ + b] + diag[0]

        @pl.when(has[side])
        def _():
            pen_copy(1 - side).wait_recv()
            for b in range(NQ):
                node = edge_rows[side] * NQ + b
                other = helm + pen_got[side, pl.ds(b, 1), :]
                inverse[node] += other + (diag[edge_rows[side]] + diag[b])
                faces[side * NQ + b] += other + diag[0]

    for a in range(NQ):
        vals = [inverse[a * NQ + b] for b in range(NQ)]
        vals[0], vals[ORDER] = join_rows(vals[0], vals[ORDER])
        for b in range(NQ):
            inverse[a * NQ + b] = 1.0 / vals[b]

    def begin(c):
        for offset in range(1, OWNERS):
            mode_copy(c, offset).wait_recv()
        local_copy(c).wait()
        for r in range(8):
            first = c * OWNERS * CHUNK + r
            rows = [
                owned[pl.ds(first + (y * 32 + block * 8), 8, stride=32), :]
                for block in range(4)
                for y in range(0, 32, 8)
            ]
            tiles = jnp.concatenate(rows, axis=0).T
            for i in range(16):
                start = (c * PADDED + i * 8) * 8 + r
                res[pl.ds(start, 8, stride=8), :] = tiles[i * 8 : i * 8 + 8]
        for a in range(NQ):
            node = c * PADDED + a * NQ
            low, high = join_rows(load(res, node), load(res, node + ORDER))
            store(res, node, low)
            store(res, node + ORDER, high)
        nodes = range(NODES)
        if c == 0:
            zero = jnp.zeros((8, 128), jnp.float32)
            for side in range(2):
                for b in range(NQ):
                    node = edge_rows[side] * NQ + b
                    sent[0, c, side, b] = -load(res, node)
                    store(res, node, zero)
                    direction[node] = zero
                    out[node] = zero
            start_faces(0, c)
            nodes = range(NQ, NODES - NQ)
        for i in nodes:
            value = inverse[i] * load(res, c * PADDED + i) * CHEBYSHEV[0][1]
            direction[c * PADDED + i] = value
            out[c * PADDED + i] = value
        prepare_edges(c)

    def update(base, node, change, keep, gain):
        now = load(res, base + node) - change
        store(res, base + node, now)
        value = keep * direction[base + node] + gain * (inverse[node] * now)
        direction[base + node] = value
        out[base + node] += value

    def finish_rhs(c):
        wait_faces(0, c)
        for side in range(2):
            for b in range(NQ):
                change = sent[0, c, side, b] + got[0, c, side, b]
                update(c * PADDED, edge_rows[side] * NQ + b, change, *CHEBYSHEV[0])

    def finish_face(step, c, side):
        keep, gain = coefficients(step)
        owners = 1.0 + has_neighbour(side).astype(jnp.float32)
        vals = [direction[c * PADDED + side * (ORDER * NQ) + b] for b in range(NQ)]
        terms = lines(vals, SCALED, 1)
        terms = [terms[b] * owners + faces[side * NQ + b] * vals[b] for b in range(NQ)]
        wait_face(step, c, side)
        for b in range(NQ):
            terms[b] = terms[b] + (sent[step, c, side, b] + got[step, c, side, b])
        terms[0], terms[ORDER] = join_rows(terms[0], terms[ORDER])
        for b in range(NQ):
            update(c * PADDED, side * (ORDER * NQ) + b, terms[b], keep, gain)

    def prepare_edges(c):
        for b in range(NQ):
            vals = [direction[c * PADDED + a * NQ + b] for a in range(1, ORDER)]
            edges[c * 2 * NQ + b], edges[c * 2 * NQ + NQ + b] = edge_lines([None] + vals + [None])

    def send_face(step, c, side):
        other = c * PADDED + (1 - side) * (ORDER * NQ)
        for b in range(NQ):
            across = direction[other + b] * float(SCALED[0, ORDER])
            sent[step, c, side, b] = edges[(c * 2 + side) * NQ + b] + across
        start_face(step, c, side)

    def interior(step, c):
        base = c * PADDED
        keep, gain = coefficients(step)

        def along_first(b, _):
            vals = [direction[base + a * NQ + b] for a in range(NQ)]
            terms = lines(vals, SCALED, 1)
            for a in range(1, ORDER):
                tmp[a * NQ + b] = terms[a] + coeff[a * NQ + b] * vals[a]
            return 0

        def along_second(a, _):
            terms = lines([direction[base + a * NQ + b] for b in range(NQ)], SCALED, 1)
            terms = [terms[b] + tmp[a * NQ + b] for b in range(NQ)]
            terms[0], terms[ORDER] = join_rows(terms[0], terms[ORDER])
            for b in range(NQ):
                update(base, a * NQ + b, terms[b], keep, gain)
            return 0

        lax.fori_loop(0, NQ, along_first, 0, unroll=UNROLL)
        lax.fori_loop(1, ORDER, along_second, 0, unroll=UNROLL)
        prepare_edges(c)

    def advance(step, c):
        send_face(step + 1, c, outer)
        interior(step + 1, c)
        finish_face(step + 1, c, outer)

    def sweep(q, _):
        step, c = q // COMPS, q % COMPS
        finish_face(step, c, inner)
        advance(step, c)
        send_face(step + 2, c, inner)
        return 0

    for c in range(COMPS):
        begin(c)
        if c == 0:
            finish_rhs(c)
        send_face(1, c, inner)
        advance(0, c)
        send_face(2, c, inner)
    lax.fori_loop(COMPS, (ITERS - 2) * COMPS, sweep, 0)
    for c in range(COMPS):
        finish_face(ITERS - 2, c, inner)
        advance(ITERS - 2, c)
    saves = []
    for c in range(COMPS):
        finish_face(ITERS - 1, c, inner)
        part = pl.ds(c * PADDED, NODES)
        saves.append(pltpu.make_async_copy(out.at[part], result.at[part], out_sem.at[c]))
        saves[-1].start()

    for c in range(COMPS):
        saves[c].wait()
        for offset in range(1, OWNERS):
            mode_copy(c, offset).wait_send()
    for side in range(2):

        @pl.when(has[side])
        def _():
            pen_copy(side).wait_send()
            for step in range(ITERS):
                for c in range(COMPS):
                    face_copy(step, c, side).wait_send()


def load(ref, node):
    return ref[pl.ds(pl.multiple_of(node * 8, 8), 8), :]


def store(ref, node, value):
    ref[pl.ds(pl.multiple_of(node * 8, 8), 8), :] = value


def run_step(velocity, penalty):
    tiles = velocity.reshape(COMPS * NODES, 2, 4, 128).transpose(0, 2, 1, 3)
    tiles = tiles.reshape(COMPS * NODES, 8, 128)
    high, low = dft_table()
    pen = penalty.reshape(NODES, 1, 32)
    tile = (8, 128)
    return pl.pallas_call(
        step_kernel,
        out_shape=jax.ShapeDtypeStruct((COMPS * PADDED,) + tile, jnp.float32),
        in_specs=[pl.BlockSpec(memory_space=pltpu.HBM)] * 4,
        out_specs=pl.BlockSpec(memory_space=pltpu.HBM),
        scratch_shapes=[
            pltpu.VMEM((COMPS * PADDED,) + tile, jnp.float32),
            pltpu.VMEM((COMPS * NODES,) + tile, jnp.float32),
            pltpu.VMEM((PLANES, PLANES), jnp.bfloat16),
            pltpu.VMEM((PLANES, PLANES), jnp.bfloat16),
            pltpu.VMEM((NODES, 1, 32), jnp.float32),
            pltpu.VMEM((PADDED, 128), jnp.float32),
            pltpu.VMEM((COMPS * 2 * NQ,) + tile, jnp.float32),
            pltpu.VMEM((2 * NQ,) + tile, jnp.float32),
            pltpu.VMEM((COMPS * PADDED * 8, 128), jnp.float32),
            pltpu.VMEM((COMPS * OWNERS * CHUNK, 128), jnp.float32),
            pltpu.VMEM((COMPS * OWNERS * CHUNK, 128), jnp.float32),
            pltpu.VMEM((COMPS * PADDED * 8, 128), jnp.float32),
            pltpu.VMEM((COMPS * PADDED,) + tile, jnp.float32),
            pltpu.VMEM((PADDED,) + tile, jnp.float32),
            pltpu.VMEM((PADDED,) + tile, jnp.float32),
            pltpu.VMEM((PADDED,) + tile, jnp.float32),
            pltpu.VMEM((ITERS, COMPS, 2, NQ) + tile, jnp.float32),
            pltpu.VMEM((ITERS, COMPS, 2, NQ) + tile, jnp.float32),
            pltpu.VMEM((2, 16, 128), jnp.float32),
            pltpu.VMEM((2, 16, 128), jnp.float32),
            pltpu.SemaphoreType.DMA((COMPS, OWNERS)),
            pltpu.SemaphoreType.DMA((COMPS, OWNERS)),
            pltpu.SemaphoreType.DMA((COMPS,)),
            pltpu.SemaphoreType.DMA((ITERS, COMPS, 2)),
            pltpu.SemaphoreType.DMA((ITERS, COMPS, 2)),
            pltpu.SemaphoreType.DMA((2,)),
            pltpu.SemaphoreType.DMA((2,)),
            pltpu.SemaphoreType.DMA((6,)),
            pltpu.SemaphoreType.DMA((COMPS,)),
        ],
        compiler_params=pltpu.CompilerParams(
            collective_id=0, has_side_effects=True, vmem_limit_bytes=VMEM_LIMIT
        ),
        name="step",
    )(tiles, jnp.asarray(high), jnp.asarray(low), pen)


def unpack_kernel(tiles_in, out, tiles, rows, load_sem, sem):
    loads = []
    for c in range(COMPS):
        part = pl.ds(c * PADDED, NODES)
        loads.append(pltpu.make_async_copy(tiles_in.at[part], tiles.at[part], load_sem.at[c]))
        loads[-1].start()
    size = 8 * COMPS * NODES
    copies = []
    for block in range(4):
        for c in range(COMPS):
            if block == 0:
                loads[c].wait()
            for node in range(NODES):
                tile = tiles[c * PADDED + node]
                if block:
                    tile = roll(tile, -32 * block)
                first = block * size + c * NODES + node
                rows[pl.ds(first, 8, stride=COMPS * NODES), :] = tile[:, :32]
        part = pl.ds(block * size, size)
        copies.append(pltpu.make_async_copy(rows.at[part], out.at[part], sem.at[block]))
        copies[-1].start()
    for copy in copies:
        copy.wait()


def unpack_output(tiles):
    shape = (32 * COMPS * NODES, 32)
    out = pl.pallas_call(
        unpack_kernel,
        out_shape=jax.ShapeDtypeStruct(shape, jnp.float32),
        in_specs=[pl.BlockSpec(memory_space=pltpu.HBM)],
        out_specs=pl.BlockSpec(memory_space=pltpu.HBM),
        scratch_shapes=[
            pltpu.VMEM(tiles.shape, jnp.float32),
            pltpu.VMEM(shape, jnp.float32),
            pltpu.SemaphoreType.DMA((COMPS,)),
            pltpu.SemaphoreType.DMA((4,)),
        ],
        compiler_params=pltpu.CompilerParams(vmem_limit_bytes=VMEM_LIMIT),
        name="unpack",
    )(tiles)
    return out.reshape(32, COMPS, NQ, NQ, 1, 32)


def per_device(velocity, penalty):
    return unpack_output(run_step(velocity, penalty))


def solution(mesh):
    return jax.shard_map(
        per_device,
        mesh=mesh,
        in_specs=(P(None, None, None, "mesh", "mode", None), P(None, None, "mesh", None)),
        out_specs=P("mode", None, None, None, "mesh", None),
        check_vma=False,
    )
```

```python
import functools
import math

import jax
import jax.numpy as jnp
import ml_dtypes
import numpy as np
from jax import lax
from jax.experimental import pallas as pl
from jax.experimental.pallas import tpu as pltpu
from jax.sharding import PartitionSpec as P

ORDER = 10
NQ = ORDER + 1
NODES = NQ * NQ
PLANES = 512
MODES = 256
ITERS = 6
HELM_BASE = 1.0
SPAN_WAVE = 0.02
BOUND_RATIO = 25.0

COMPS = 3
PADDED = 128
OWNERS = 16
COLUMNS = 8
CHUNK = 64
HALF = ORDER // 2
UNROLL = True
MESH = pl.DeviceIdType.MESH
VMEM_LIMIT = 60 * 2**20


def legendre_pair(points, order):
    previous = points * 0.0 + 1.0
    current = points * 1.0
    for degree in range(2, order + 1):
        following = ((2 * degree - 1) * points * current - (degree - 1) * previous) / degree
        previous = current
        current = following
    return (current, previous)


def gll_tables(order):
    count = order + 1
    points = -np.cos(np.pi * np.arange(count) / order)
    for sweep in range(200):
        top_vals, below_vals = legendre_pair(points, order)
        points = points - (points * top_vals - below_vals) / (count * top_vals)
    legendre_vals, below_vals = legendre_pair(points, order)
    weights = 2.0 / (order * (order + 1) * legendre_vals**2)
    identity = np.eye(count)
    spacing = points[:, None] - points[None, :] + identity
    derivative = legendre_vals[:, None] / (legendre_vals[None, :] * spacing) * (1.0 - identity)
    corner = np.concatenate(
        [[-order * (order + 1) / 4.0], np.zeros(order - 1), [order * (order + 1) / 4.0]]
    )
    derivative = derivative + identity * corner[None, :]
    stiffness = derivative.T @ (weights[:, None] * derivative)
    weight_mat = identity * weights[None, :]
    laplace = np.kron(stiffness, weight_mat) + np.kron(weight_mat, stiffness)
    upper_bound = float(
        np.max(np.sum(np.abs(laplace), axis=1) / np.sum(laplace * np.eye(count * count), axis=1))
    )
    return weights, stiffness, derivative, upper_bound


WEIGHTS, STIFF, DERIV, TOP = gll_tables(ORDER)
SCALED = STIFF / WEIGHTS[:, None]


def chebyshev_table():
    low = TOP / BOUND_RATIO
    mid = (TOP + low) / 2.0
    half = (TOP - low) / 2.0
    table = [(0.0, 1.0 / mid)]
    recurrence = half / mid
    for step in range(ITERS - 1):
        following = 1.0 / (2.0 * mid / half - recurrence)
        table.append((following * recurrence, 2.0 * following / half))
        recurrence = following
    return table


CHEBYSHEV = chebyshev_table()


def coefficients(step):
    keep, gain = CHEBYSHEV[0]
    for i in range(1, ITERS):
        keep = jnp.where(step == i, CHEBYSHEV[i][0], keep)
        gain = jnp.where(step == i, CHEBYSHEV[i][1], gain)
    return keep, gain


def dft_table():
    planes = np.arange(PLANES)
    modes = np.arange(MODES)
    angles = 2.0 * np.pi / PLANES * (modes[:, None] * planes[None, :] % PLANES)
    table = np.concatenate([np.cos(angles), -np.sin(angles)]) / math.sqrt(PLANES)
    high = table.astype(ml_dtypes.bfloat16)
    low = (table - high.astype(np.float64)).astype(ml_dtypes.bfloat16)
    return high, low


def lines(vals, matrix, sign):
    evens = [vals[k] + vals[ORDER - k] for k in range(HALF)]
    odds = [vals[k] - vals[ORDER - k] for k in range(HALF)]
    out = [None] * NQ
    for i in range(HALF):
        even = vals[HALF] * float(matrix[i, HALF])
        odd = None
        for k in range(HALF):
            even = even + evens[k] * float((matrix[i, k] + matrix[i, ORDER - k]) / 2)
            term = odds[k] * float((matrix[i, k] - matrix[i, ORDER - k]) / 2)
            odd = term if odd is None else odd + term
        out[i] = even + odd
        out[ORDER - i] = even - odd if sign > 0 else odd - even
    middle = vals[HALF] * float(matrix[HALF, HALF]) if sign > 0 else None
    for k in range(HALF):
        term = (evens if sign > 0 else odds)[k] * float(matrix[HALF, k])
        middle = term if middle is None else middle + term
    out[HALF] = middle
    return out


def edge_lines(vals):
    even = vals[HALF] * float(SCALED[0, HALF])
    odd = None
    for k in range(1, HALF):
        near, far = float(SCALED[0, k]), float(SCALED[0, ORDER - k])
        even = even + (vals[k] + vals[ORDER - k]) * ((near + far) / 2)
        term = (vals[k] - vals[ORDER - k]) * ((near - far) / 2)
        odd = term if odd is None else odd + term
    return even + odd, even - odd


def roll(tile, by):
    return pltpu.roll(tile, by % 128, 1)


def join_rows(low, high):
    row = lax.broadcasted_iota(jnp.int32, (8, 128), 1) % 32
    above = jnp.where(row == 31, 0.0, roll(low, -1))
    below = jnp.where(row == 0, 0.0, roll(high, 1))
    return low + below, high + above


def step_kernel(
    vel_in,
    high_in,
    low_in,
    pen_in,
    result,
    out,
    vel,
    high,
    low,
    pen_rows,
    penalty,
    edges,
    forcing,
    spectra,
    owned,
    res,
    direction,
    tmp,
    inverse,
    coeff,
    sent,
    got,
    pen_sent,
    pen_got,
    mode_send_sem,
    mode_recv_sem,
    local_sem,
    send_sem,
    recv_sem,
    pen_send_sem,
    pen_recv_sem,
    load_sem,
    out_sem,
):
    mode, column = lax.axis_index("mode"), lax.axis_index("mesh")
    has = (column > 0, column < COLUMNS - 1)
    partner = (jnp.maximum(column - 1, 0), jnp.minimum(column + 1, COLUMNS - 1))
    edge_rows = (0, ORDER)

    loads = [
        pltpu.make_async_copy(
            vel_in.at[pl.ds(c * NODES, NODES)], vel.at[pl.ds(c * NODES, NODES)], load_sem.at[c]
        )
        for c in range(COMPS)
    ]
    load_high = pltpu.make_async_copy(high_in, high, load_sem.at[3])
    load_low = pltpu.make_async_copy(low_in, low, load_sem.at[4])
    load_pen = pltpu.make_async_copy(pen_in, pen_rows, load_sem.at[5])
    for copy in [loads[0], loads[1], loads[2], load_high, load_low, load_pen]:
        copy.start()

    def chunk(c, owner):
        return pl.ds(pl.multiple_of((c * OWNERS + owner) * CHUNK, CHUNK), CHUNK)

    def mode_copy(c, offset):
        dest = lax.rem(mode + offset, OWNERS)
        return pltpu.make_async_remote_copy(
            src_ref=spectra.at[chunk(c, dest)],
            dst_ref=owned.at[chunk(c, mode)],
            send_sem=mode_send_sem.at[c, offset],
            recv_sem=mode_recv_sem.at[c, offset],
            device_id=(dest, column),
            device_id_type=MESH,
        )

    def local_copy(c):
        return pltpu.make_async_copy(
            spectra.at[chunk(c, mode)], owned.at[chunk(c, mode)], local_sem.at[c]
        )

    def face_copy(step, c, side):
        return pltpu.make_async_remote_copy(
            src_ref=sent.at[step, c, side],
            dst_ref=got.at[step, c, 1 - side],
            send_sem=send_sem.at[step, c, side],
            recv_sem=recv_sem.at[step, c, 1 - side],
            device_id=(mode, partner[side]),
            device_id_type=MESH,
        )

    def pen_copy(side):
        return pltpu.make_async_remote_copy(
            src_ref=pen_sent.at[side],
            dst_ref=pen_got.at[1 - side],
            send_sem=pen_send_sem.at[side],
            recv_sem=pen_recv_sem.at[1 - side],
            device_id=(mode, partner[side]),
            device_id_type=MESH,
        )

    def start_faces(step, c):
        for side in range(2):

            @pl.when(has[side])
            def _():
                face_copy(step, c, side).start()

    def wait_faces(step, c):
        for side in range(2):

            @pl.when(has[side])
            def _():
                face_copy(step, c, 1 - side).wait_recv()

    for side in range(2):

        @pl.when(jnp.logical_not(has[side]))
        def _():
            for step in range(ITERS):
                got[step, :, side] = jnp.zeros((COMPS, NQ, 8, 128), jnp.float32)

    barrier = pltpu.get_barrier_semaphore()
    for offset in range(1, OWNERS):
        dest = lax.rem(mode + offset, OWNERS)
        pl.semaphore_signal(barrier, inc=1, device_id=(dest, column), device_id_type=MESH)
    for side in range(2):

        @pl.when(has[side])
        def _():
            pl.semaphore_signal(
                barrier, inc=1, device_id=(mode, partner[side]), device_id_type=MESH
            )

    def node_rows(c, node):
        return pl.ds(pl.multiple_of((c * PADDED + node) * 8, 8), 8)

    def advect(c):
        pad = pl.ds((c * PADDED + NODES) * 8, (PADDED - NODES) * 8)
        forcing[pad, :] = jnp.zeros(((PADDED - NODES) * 8, 128), jnp.float32)

        def advect_first(b, _):
            grads = lines([vel[c * NODES + a * NQ + b] for a in range(NQ)], DERIV, -1)
            for a in range(NQ):
                tmp[a * NQ + b] = vel[a * NQ + b] * grads[a]
            return 0

        def advect_second(a, _):
            vals = [vel[c * NODES + a * NQ + b] for b in range(NQ)]
            grads = lines(vals, DERIV, -1)
            for b in range(NQ):
                node = a * NQ + b
                value = vals[b] - (tmp[node] + vel[NODES + node] * grads[b])
                forcing[node_rows(c, node), :] = value
            return 0

        lax.fori_loop(0, NQ, advect_first, 0, unroll=UNROLL)
        lax.fori_loop(0, NQ, advect_second, 0, unroll=UNROLL)

    def send_forcing_faces(c):
        for side in range(2):
            for b in range(NQ):
                sent[0, c, side, b] = forcing[node_rows(c, edge_rows[side] * NQ + b), :]
        start_faces(0, c)

    def add_forcing_faces(c):
        wait_faces(0, c)
        for side in range(2):
            for b in range(NQ):
                forcing[node_rows(c, edge_rows[side] * NQ + b), :] += got[0, c, side, b]

    def transform(c):
        field = jnp.concatenate(
            [
                jnp.concatenate(
                    [
                        forcing[pl.ds(c * PADDED * 8 + t * 2 + y, PADDED, stride=8), :]
                        for y in range(2)
                    ],
                    axis=0,
                )
                for t in range(4)
            ],
            axis=1,
        )
        upper = field.astype(jnp.bfloat16)
        lower = (field - upper.astype(jnp.float32)).astype(jnp.bfloat16)
        dot = functools.partial(
            lax.dot_general,
            dimension_numbers=(((1,), (1,)), ((), ())),
            preferred_element_type=jnp.float32,
        )
        modes = dot(high[...], upper) + (dot(high[...], lower) + dot(low[...], upper))
        for owner in range(OWNERS):
            for y in range(2):
                spectra[pl.ds((c * OWNERS + owner) * CHUNK + y * 32, 32), :] = modes[
                    owner * 32 : owner * 32 + 32, y * 128 : y * 128 + 128
                ]
        for offset in range(1, OWNERS):
            mode_copy(c, offset).start()
        local_copy(c).start()

    loads[0].wait()
    loads[1].wait()
    advect(1)
    peers = OWNERS - 1 + has[0].astype(jnp.int32) + has[1].astype(jnp.int32)
    pl.semaphore_wait(barrier, peers)
    send_forcing_faces(1)
    loads[2].wait()
    advect(2)
    send_forcing_faces(2)
    advect(0)
    load_high.wait()
    load_low.wait()
    transform(0)

    load_pen.wait()
    for node in range(NODES):
        line = pen_rows[node]
        penalty[pl.ds(node, 1), :] = jnp.concatenate([line] * 4, axis=1)
    for side in range(2):
        for b in range(NQ):
            node = edge_rows[side] * NQ + b
            pen_sent[side, pl.ds(b, 1), :] = penalty[pl.ds(node, 1), :]
        pen_sent[side, pl.ds(NQ, 16 - NQ), :] = jnp.zeros((16 - NQ, 128), jnp.float32)

        @pl.when(has[side])
        def _():
            pen_copy(side).start()

    block = lax.broadcasted_iota(jnp.int32, (8, 128), 1) // 32
    row = mode * 32 + block * 8 + lax.broadcasted_iota(jnp.int32, (8, 128), 0)
    wave = (row % MODES).astype(jnp.float32)
    helm = HELM_BASE + (SPAN_WAVE * wave) * (SPAN_WAVE * wave)

    diag = [float(SCALED[i, i]) for i in range(NQ)]
    for a in range(NQ):
        for b in range(NQ):
            value = helm + penalty[pl.ds(a * NQ + b, 1), :]
            coeff[a * NQ + b] = value
            inverse[a * NQ + b] = value + (diag[a] + diag[b])

    add_forcing_faces(1)
    transform(1)
    add_forcing_faces(2)
    transform(2)

    for side in range(2):

        @pl.when(has[side])
        def _():
            pen_copy(1 - side).wait_recv()
            for b in range(NQ):
                node = edge_rows[side] * NQ + b
                other = helm + pen_got[side, pl.ds(b, 1), :]
                inverse[node] += other + (diag[edge_rows[side]] + diag[b])

    for a in range(NQ):
        vals = [inverse[a * NQ + b] for b in range(NQ)]
        vals[0], vals[ORDER] = join_rows(vals[0], vals[ORDER])
        for b in range(NQ):
            inverse[a * NQ + b] = 1.0 / vals[b]

    def begin(c):
        for offset in range(1, OWNERS):
            mode_copy(c, offset).wait_recv()
        local_copy(c).wait()
        for r in range(8):
            first = c * OWNERS * CHUNK + r
            rows = [
                owned[pl.ds(first + (y * 32 + block * 8), 8, stride=32), :]
                for block in range(4)
                for y in range(0, 32, 8)
            ]
            tiles = jnp.concatenate(rows, axis=0).T
            for i in range(16):
                start = (c * PADDED + i * 8) * 8 + r
                res[pl.ds(start, 8, stride=8), :] = tiles[i * 8 : i * 8 + 8]
        for a in range(NQ):
            node = c * PADDED + a * NQ
            low, high = join_rows(load(res, node), load(res, node + ORDER))
            store(res, node, low)
            store(res, node + ORDER, high)
        nodes = range(NODES)
        if c == 0:
            zero = jnp.zeros((8, 128), jnp.float32)
            for side in range(2):
                for b in range(NQ):
                    node = edge_rows[side] * NQ + b
                    sent[0, c, side, b] = -load(res, node)
                    store(res, node, zero)
                    direction[node] = zero
                    out[node] = zero
            start_faces(0, c)
            nodes = range(NQ, NODES - NQ)
        for i in nodes:
            value = inverse[i] * load(res, c * PADDED + i) * CHEBYSHEV[0][1]
            direction[c * PADDED + i] = value
            out[c * PADDED + i] = value
        prepare_edges(c)

    def update(base, node, change, keep, gain):
        now = load(res, base + node) - change
        store(res, base + node, now)
        value = keep * direction[base + node] + gain * (inverse[node] * now)
        direction[base + node] = value
        out[base + node] += value

    def finish_faces(step, c):
        wait_faces(step, c)
        keep, gain = coefficients(step)
        for side in range(2):
            for b in range(NQ):
                change = sent[step, c, side, b] + got[step, c, side, b]
                update(c * PADDED, edge_rows[side] * NQ + b, change, keep, gain)

    def prepare_edges(c):
        for b in range(NQ):
            vals = [direction[c * PADDED + a * NQ + b] for a in range(1, ORDER)]
            edges[c * 2 * NQ + b], edges[c * 2 * NQ + NQ + b] = edge_lines([None] + vals + [None])

    def send_edges(step, c):
        base = c * PADDED
        own, across = float(SCALED[0, 0]), float(SCALED[0, ORDER])
        for side in range(2):
            node = edge_rows[side] * NQ
            other = edge_rows[1 - side] * NQ
            vals = [direction[base + node + b] for b in range(NQ)]
            terms = lines(vals, SCALED, 1)
            for b in range(NQ):
                first = edges[c * 2 * NQ + side * NQ + b] + direction[base + other + b] * across
                terms[b] = terms[b] + first + vals[b] * (coeff[node + b] + own)
            terms[0], terms[ORDER] = join_rows(terms[0], terms[ORDER])
            for b in range(NQ):
                sent[step, c, side, b] = terms[b]
        start_faces(step, c)

    def interior(step, c):
        base = c * PADDED
        keep, gain = coefficients(step)

        def along_first(b, _):
            vals = [direction[base + a * NQ + b] for a in range(NQ)]
            terms = lines(vals, SCALED, 1)
            for a in range(1, ORDER):
                tmp[a * NQ + b] = terms[a] + coeff[a * NQ + b] * vals[a]
            return 0

        def along_second(a, _):
            terms = lines([direction[base + a * NQ + b] for b in range(NQ)], SCALED, 1)
            terms = [terms[b] + tmp[a * NQ + b] for b in range(NQ)]
            terms[0], terms[ORDER] = join_rows(terms[0], terms[ORDER])
            for b in range(NQ):
                update(base, a * NQ + b, terms[b], keep, gain)
            return 0

        lax.fori_loop(0, NQ, along_first, 0, unroll=UNROLL)
        lax.fori_loop(1, ORDER, along_second, 0, unroll=UNROLL)
        prepare_edges(c)

    def sweep(q, _):
        step, c = q // COMPS, q % COMPS
        finish_faces(step, c)
        send_edges(step + 1, c)
        interior(step + 1, c)
        return 0

    begin(0)
    finish_faces(0, 0)
    for c in range(COMPS):
        send_edges(1, c)
        interior(1, c)
        if c + 1 < COMPS:
            begin(c + 1)
    lax.fori_loop(COMPS, (ITERS - 1) * COMPS, sweep, 0)
    saves = []
    for c in range(COMPS):
        finish_faces(ITERS - 1, c)
        part = pl.ds(c * PADDED, NODES)
        saves.append(pltpu.make_async_copy(out.at[part], result.at[part], out_sem.at[c]))
        saves[-1].start()

    for c in range(COMPS):
        saves[c].wait()
        for offset in range(1, OWNERS):
            mode_copy(c, offset).wait_send()
    for side in range(2):

        @pl.when(has[side])
        def _():
            pen_copy(side).wait_send()
            for step in range(ITERS):
                for c in range(COMPS):
                    face_copy(step, c, side).wait_send()


def load(ref, node):
    return ref[pl.ds(pl.multiple_of(node * 8, 8), 8), :]


def store(ref, node, value):
    ref[pl.ds(pl.multiple_of(node * 8, 8), 8), :] = value


def run_step(velocity, penalty):
    tiles = velocity.reshape(COMPS * NODES, 2, 4, 128).transpose(0, 2, 1, 3)
    tiles = tiles.reshape(COMPS * NODES, 8, 128)
    high, low = dft_table()
    pen = penalty.reshape(NODES, 1, 32)
    tile = (8, 128)
    return pl.pallas_call(
        step_kernel,
        out_shape=jax.ShapeDtypeStruct((COMPS * PADDED,) + tile, jnp.float32),
        in_specs=[pl.BlockSpec(memory_space=pltpu.HBM)] * 4,
        out_specs=pl.BlockSpec(memory_space=pltpu.HBM),
        scratch_shapes=[
            pltpu.VMEM((COMPS * PADDED,) + tile, jnp.float32),
            pltpu.VMEM((COMPS * NODES,) + tile, jnp.float32),
            pltpu.VMEM((PLANES, PLANES), jnp.bfloat16),
            pltpu.VMEM((PLANES, PLANES), jnp.bfloat16),
            pltpu.VMEM((NODES, 1, 32), jnp.float32),
            pltpu.VMEM((PADDED, 128), jnp.float32),
            pltpu.VMEM((COMPS * 2 * NQ,) + tile, jnp.float32),
            pltpu.VMEM((COMPS * PADDED * 8, 128), jnp.float32),
            pltpu.VMEM((COMPS * OWNERS * CHUNK, 128), jnp.float32),
            pltpu.VMEM((COMPS * OWNERS * CHUNK, 128), jnp.float32),
            pltpu.VMEM((COMPS * PADDED * 8, 128), jnp.float32),
            pltpu.VMEM((COMPS * PADDED,) + tile, jnp.float32),
            pltpu.VMEM((PADDED,) + tile, jnp.float32),
            pltpu.VMEM((PADDED,) + tile, jnp.float32),
            pltpu.VMEM((PADDED,) + tile, jnp.float32),
            pltpu.VMEM((ITERS, COMPS, 2, NQ) + tile, jnp.float32),
            pltpu.VMEM((ITERS, COMPS, 2, NQ) + tile, jnp.float32),
            pltpu.VMEM((2, 16, 128), jnp.float32),
            pltpu.VMEM((2, 16, 128), jnp.float32),
            pltpu.SemaphoreType.DMA((COMPS, OWNERS)),
            pltpu.SemaphoreType.DMA((COMPS, OWNERS)),
            pltpu.SemaphoreType.DMA((COMPS,)),
            pltpu.SemaphoreType.DMA((ITERS, COMPS, 2)),
            pltpu.SemaphoreType.DMA((ITERS, COMPS, 2)),
            pltpu.SemaphoreType.DMA((2,)),
            pltpu.SemaphoreType.DMA((2,)),
            pltpu.SemaphoreType.DMA((6,)),
            pltpu.SemaphoreType.DMA((COMPS,)),
        ],
        compiler_params=pltpu.CompilerParams(
            collective_id=0, has_side_effects=True, vmem_limit_bytes=VMEM_LIMIT
        ),
        name="step",
    )(tiles, jnp.asarray(high), jnp.asarray(low), pen)


def unpack_kernel(tiles_in, out, tiles, rows, load_sem, sem):
    loads = []
    for c in range(COMPS):
        part = pl.ds(c * PADDED, NODES)
        loads.append(pltpu.make_async_copy(tiles_in.at[part], tiles.at[part], load_sem.at[c]))
        loads[-1].start()
    size = 8 * COMPS * NODES
    copies = []
    for block in range(4):
        for c in range(COMPS):
            if block == 0:
                loads[c].wait()
            for node in range(NODES):
                tile = tiles[c * PADDED + node]
                if block:
                    tile = roll(tile, -32 * block)
                first = block * size + c * NODES + node
                rows[pl.ds(first, 8, stride=COMPS * NODES), :] = tile[:, :32]
        part = pl.ds(block * size, size)
        copies.append(pltpu.make_async_copy(rows.at[part], out.at[part], sem.at[block]))
        copies[-1].start()
    for copy in copies:
        copy.wait()


def unpack_output(tiles):
    shape = (32 * COMPS * NODES, 32)
    out = pl.pallas_call(
        unpack_kernel,
        out_shape=jax.ShapeDtypeStruct(shape, jnp.float32),
        in_specs=[pl.BlockSpec(memory_space=pltpu.HBM)],
        out_specs=pl.BlockSpec(memory_space=pltpu.HBM),
        scratch_shapes=[
            pltpu.VMEM(tiles.shape, jnp.float32),
            pltpu.VMEM(shape, jnp.float32),
            pltpu.SemaphoreType.DMA((COMPS,)),
            pltpu.SemaphoreType.DMA((4,)),
        ],
        compiler_params=pltpu.CompilerParams(vmem_limit_bytes=VMEM_LIMIT),
        name="unpack",
    )(tiles)
    return out.reshape(32, COMPS, NQ, NQ, 1, 32)


def per_device(velocity, penalty):
    return unpack_output(run_step(velocity, penalty))


def solution(mesh):
    return jax.shard_map(
        per_device,
        mesh=mesh,
        in_specs=(P(None, None, None, "mesh", "mode", None), P(None, None, "mesh", None)),
        out_specs=P("mode", None, None, None, "mesh", None),
        check_vma=False,
    )
```

```python
import functools
import math

import jax
import jax.numpy as jnp
import ml_dtypes
import numpy as np
from jax import lax
from jax.experimental import pallas as pl
from jax.experimental.pallas import tpu as pltpu
from jax.sharding import PartitionSpec as P

ORDER = 10
NQ = ORDER + 1
NODES = NQ * NQ
PLANES = 512
MODES = 256
ITERS = 6
HELM_BASE = 1.0
SPAN_WAVE = 0.02
BOUND_RATIO = 25.0

COMPS = 3
PADDED = 128
OWNERS = 16
COLUMNS = 8
CHUNK = 64
HALF = ORDER // 2
UNROLL = True
MESH = pl.DeviceIdType.MESH
VMEM_LIMIT = 60 * 2**20


def legendre_pair(points, order):
    previous = points * 0.0 + 1.0
    current = points * 1.0
    for degree in range(2, order + 1):
        following = ((2 * degree - 1) * points * current - (degree - 1) * previous) / degree
        previous = current
        current = following
    return (current, previous)


def gll_tables(order):
    count = order + 1
    points = -np.cos(np.pi * np.arange(count) / order)
    for sweep in range(200):
        top_vals, below_vals = legendre_pair(points, order)
        points = points - (points * top_vals - below_vals) / (count * top_vals)
    legendre_vals, below_vals = legendre_pair(points, order)
    weights = 2.0 / (order * (order + 1) * legendre_vals**2)
    identity = np.eye(count)
    spacing = points[:, None] - points[None, :] + identity
    derivative = legendre_vals[:, None] / (legendre_vals[None, :] * spacing) * (1.0 - identity)
    corner = np.concatenate(
        [[-order * (order + 1) / 4.0], np.zeros(order - 1), [order * (order + 1) / 4.0]]
    )
    derivative = derivative + identity * corner[None, :]
    stiffness = derivative.T @ (weights[:, None] * derivative)
    weight_mat = identity * weights[None, :]
    laplace = np.kron(stiffness, weight_mat) + np.kron(weight_mat, stiffness)
    upper_bound = float(
        np.max(np.sum(np.abs(laplace), axis=1) / np.sum(laplace * np.eye(count * count), axis=1))
    )
    return weights, stiffness, derivative, upper_bound


WEIGHTS, STIFF, DERIV, TOP = gll_tables(ORDER)
SCALED = STIFF / WEIGHTS[:, None]


def chebyshev_table():
    low = TOP / BOUND_RATIO
    mid = (TOP + low) / 2.0
    half = (TOP - low) / 2.0
    table = [(0.0, 1.0 / mid)]
    recurrence = half / mid
    for step in range(ITERS - 1):
        following = 1.0 / (2.0 * mid / half - recurrence)
        table.append((following * recurrence, 2.0 * following / half))
        recurrence = following
    return table


CHEBYSHEV = chebyshev_table()


def coefficients(step):
    keep, gain = CHEBYSHEV[0]
    for i in range(1, ITERS):
        keep = jnp.where(step == i, CHEBYSHEV[i][0], keep)
        gain = jnp.where(step == i, CHEBYSHEV[i][1], gain)
    return keep, gain


def dft_table():
    planes = np.arange(PLANES)
    modes = np.arange(MODES)
    angles = 2.0 * np.pi / PLANES * (modes[:, None] * planes[None, :] % PLANES)
    table = np.concatenate([np.cos(angles), -np.sin(angles)]) / math.sqrt(PLANES)
    high = table.astype(ml_dtypes.bfloat16)
    low = (table - high.astype(np.float64)).astype(ml_dtypes.bfloat16)
    return high, low


def lines(vals, matrix, sign):
    evens = [vals[k] + vals[ORDER - k] for k in range(HALF)]
    odds = [vals[k] - vals[ORDER - k] for k in range(HALF)]
    out = [None] * NQ
    for i in range(HALF):
        even = vals[HALF] * float(matrix[i, HALF])
        odd = None
        for k in range(HALF):
            even = even + evens[k] * float((matrix[i, k] + matrix[i, ORDER - k]) / 2)
            term = odds[k] * float((matrix[i, k] - matrix[i, ORDER - k]) / 2)
            odd = term if odd is None else odd + term
        out[i] = even + odd
        out[ORDER - i] = even - odd if sign > 0 else odd - even
    middle = vals[HALF] * float(matrix[HALF, HALF]) if sign > 0 else None
    for k in range(HALF):
        term = (evens if sign > 0 else odds)[k] * float(matrix[HALF, k])
        middle = term if middle is None else middle + term
    out[HALF] = middle
    return out


def edge_lines(vals):
    even = vals[HALF] * float(SCALED[0, HALF])
    odd = None
    for k in range(1, HALF):
        near, far = float(SCALED[0, k]), float(SCALED[0, ORDER - k])
        even = even + (vals[k] + vals[ORDER - k]) * ((near + far) / 2)
        term = (vals[k] - vals[ORDER - k]) * ((near - far) / 2)
        odd = term if odd is None else odd + term
    return even + odd, even - odd


def roll(tile, by):
    return pltpu.roll(tile, by % 128, 1)


def join_rows(low, high):
    row = lax.broadcasted_iota(jnp.int32, (8, 128), 1) % 32
    above = jnp.where(row == 31, 0.0, roll(low, -1))
    below = jnp.where(row == 0, 0.0, roll(high, 1))
    return low + below, high + above


def step_kernel(
    vel_in,
    high_in,
    low_in,
    pen_in,
    result,
    out,
    vel,
    high,
    low,
    pen_rows,
    penalty,
    edges,
    forcing,
    spectra,
    owned,
    res,
    direction,
    tmp,
    inverse,
    coeff,
    sent,
    got,
    pen_sent,
    pen_got,
    mode_send_sem,
    mode_recv_sem,
    local_sem,
    send_sem,
    recv_sem,
    pen_send_sem,
    pen_recv_sem,
    load_sem,
    out_sem,
):
    mode, column = lax.axis_index("mode"), lax.axis_index("mesh")
    has = (column > 0, column < COLUMNS - 1)
    partner = (jnp.maximum(column - 1, 0), jnp.minimum(column + 1, COLUMNS - 1))
    edge_rows = (0, ORDER)

    loads = [
        pltpu.make_async_copy(
            vel_in.at[pl.ds(c * NODES, NODES)], vel.at[pl.ds(c * NODES, NODES)], load_sem.at[c]
        )
        for c in range(COMPS)
    ]
    load_high = pltpu.make_async_copy(high_in, high, load_sem.at[3])
    load_low = pltpu.make_async_copy(low_in, low, load_sem.at[4])
    load_pen = pltpu.make_async_copy(pen_in, pen_rows, load_sem.at[5])
    for copy in [loads[0], loads[1], loads[2], load_high, load_low, load_pen]:
        copy.start()

    def chunk(c, owner):
        return pl.ds(pl.multiple_of((c * OWNERS + owner) * CHUNK, CHUNK), CHUNK)

    def mode_copy(c, offset):
        dest = lax.rem(mode + offset, OWNERS)
        return pltpu.make_async_remote_copy(
            src_ref=spectra.at[chunk(c, dest)],
            dst_ref=owned.at[chunk(c, mode)],
            send_sem=mode_send_sem.at[c, offset],
            recv_sem=mode_recv_sem.at[c, offset],
            device_id=(dest, column),
            device_id_type=MESH,
        )

    def local_copy(c):
        return pltpu.make_async_copy(
            spectra.at[chunk(c, mode)], owned.at[chunk(c, mode)], local_sem.at[c]
        )

    def face_copy(step, c, side):
        return pltpu.make_async_remote_copy(
            src_ref=sent.at[step, c, side],
            dst_ref=got.at[step, c, 1 - side],
            send_sem=send_sem.at[step, c, side],
            recv_sem=recv_sem.at[step, c, 1 - side],
            device_id=(mode, partner[side]),
            device_id_type=MESH,
        )

    def pen_copy(side):
        return pltpu.make_async_remote_copy(
            src_ref=pen_sent.at[side],
            dst_ref=pen_got.at[1 - side],
            send_sem=pen_send_sem.at[side],
            recv_sem=pen_recv_sem.at[1 - side],
            device_id=(mode, partner[side]),
            device_id_type=MESH,
        )

    def start_face(step, c, side):
        @pl.when(has[side])
        def _():
            face_copy(step, c, side).start()

    def wait_face(step, c, side):
        @pl.when(has[side])
        def _():
            face_copy(step, c, 1 - side).wait_recv()

    for side in range(2):

        @pl.when(jnp.logical_not(has[side]))
        def _():
            for step in range(ITERS):
                got[step, :, side] = jnp.zeros((COMPS, NQ, 8, 128), jnp.float32)

    barrier = pltpu.get_barrier_semaphore()
    for offset in range(1, OWNERS):
        dest = lax.rem(mode + offset, OWNERS)
        pl.semaphore_signal(barrier, inc=1, device_id=(dest, column), device_id_type=MESH)
    for side in range(2):

        @pl.when(has[side])
        def _():
            pl.semaphore_signal(
                barrier, inc=1, device_id=(mode, partner[side]), device_id_type=MESH
            )

    def node_rows(c, node):
        return pl.ds(pl.multiple_of((c * PADDED + node) * 8, 8), 8)

    def advect(c):
        pad = pl.ds((c * PADDED + NODES) * 8, (PADDED - NODES) * 8)
        forcing[pad, :] = jnp.zeros(((PADDED - NODES) * 8, 128), jnp.float32)

        def advect_first(b, _):
            grads = lines([vel[c * NODES + a * NQ + b] for a in range(NQ)], DERIV, -1)
            for a in range(NQ):
                tmp[a * NQ + b] = vel[a * NQ + b] * grads[a]
            return 0

        def advect_second(a, _):
            vals = [vel[c * NODES + a * NQ + b] for b in range(NQ)]
            grads = lines(vals, DERIV, -1)
            for b in range(NQ):
                node = a * NQ + b
                value = vals[b] - (tmp[node] + vel[NODES + node] * grads[b])
                forcing[node_rows(c, node), :] = value
            return 0

        lax.fori_loop(0, NQ, advect_first, 0, unroll=UNROLL)
        lax.fori_loop(0, NQ, advect_second, 0, unroll=UNROLL)

    def send_forcing_faces(c):
        for side in range(2):
            for b in range(NQ):
                sent[0, c, side, b] = forcing[node_rows(c, edge_rows[side] * NQ + b), :]
            start_face(0, c, side)

    def add_forcing_faces(c):
        for side in range(2):
            wait_face(0, c, side)
            for b in range(NQ):
                forcing[node_rows(c, edge_rows[side] * NQ + b), :] += got[0, c, side, b]

    def transform(c):
        field = jnp.concatenate(
            [
                jnp.concatenate(
                    [
                        forcing[pl.ds(c * PADDED * 8 + t * 2 + y, PADDED, stride=8), :]
                        for y in range(2)
                    ],
                    axis=0,
                )
                for t in range(4)
            ],
            axis=1,
        )
        upper = field.astype(jnp.bfloat16)
        lower = (field - upper.astype(jnp.float32)).astype(jnp.bfloat16)
        dot = functools.partial(
            lax.dot_general,
            dimension_numbers=(((1,), (1,)), ((), ())),
            preferred_element_type=jnp.float32,
        )
        modes = dot(high[...], upper) + (dot(high[...], lower) + dot(low[...], upper))
        for owner in range(OWNERS):
            for y in range(2):
                spectra[pl.ds((c * OWNERS + owner) * CHUNK + y * 32, 32), :] = modes[
                    owner * 32 : owner * 32 + 32, y * 128 : y * 128 + 128
                ]
        for offset in range(1, OWNERS):
            mode_copy(c, offset).start()
        local_copy(c).start()

    loads[0].wait()
    loads[1].wait()
    advect(1)
    peers = OWNERS - 1 + has[0].astype(jnp.int32) + has[1].astype(jnp.int32)
    pl.semaphore_wait(barrier, peers)
    send_forcing_faces(1)
    loads[2].wait()
    advect(2)
    send_forcing_faces(2)
    advect(0)
    load_high.wait()
    load_low.wait()
    transform(0)

    load_pen.wait()
    for node in range(NODES):
        line = pen_rows[node]
        penalty[pl.ds(node, 1), :] = jnp.concatenate([line] * 4, axis=1)
    for side in range(2):
        for b in range(NQ):
            node = edge_rows[side] * NQ + b
            pen_sent[side, pl.ds(b, 1), :] = penalty[pl.ds(node, 1), :]
        pen_sent[side, pl.ds(NQ, 16 - NQ), :] = jnp.zeros((16 - NQ, 128), jnp.float32)

        @pl.when(has[side])
        def _():
            pen_copy(side).start()

    block = lax.broadcasted_iota(jnp.int32, (8, 128), 1) // 32
    row = mode * 32 + block * 8 + lax.broadcasted_iota(jnp.int32, (8, 128), 0)
    wave = (row % MODES).astype(jnp.float32)
    helm = HELM_BASE + (SPAN_WAVE * wave) * (SPAN_WAVE * wave)

    diag = [float(SCALED[i, i]) for i in range(NQ)]
    for a in range(NQ):
        for b in range(NQ):
            value = helm + penalty[pl.ds(a * NQ + b, 1), :]
            coeff[a * NQ + b] = value
            inverse[a * NQ + b] = value + (diag[a] + diag[b])

    add_forcing_faces(1)
    transform(1)
    add_forcing_faces(2)
    transform(2)

    for side in range(2):

        @pl.when(has[side])
        def _():
            pen_copy(1 - side).wait_recv()
            for b in range(NQ):
                node = edge_rows[side] * NQ + b
                other = helm + pen_got[side, pl.ds(b, 1), :]
                inverse[node] += other + (diag[edge_rows[side]] + diag[b])

    for a in range(NQ):
        vals = [inverse[a * NQ + b] for b in range(NQ)]
        vals[0], vals[ORDER] = join_rows(vals[0], vals[ORDER])
        for b in range(NQ):
            inverse[a * NQ + b] = 1.0 / vals[b]

    def begin(c):
        for offset in range(1, OWNERS):
            mode_copy(c, offset).wait_recv()
        local_copy(c).wait()
        for r in range(8):
            first = c * OWNERS * CHUNK + r
            rows = [
                owned[pl.ds(first + (y * 32 + block * 8), 8, stride=32), :]
                for block in range(4)
                for y in range(0, 32, 8)
            ]
            tiles = jnp.concatenate(rows, axis=0).T
            for i in range(16):
                start = (c * PADDED + i * 8) * 8 + r
                res[pl.ds(start, 8, stride=8), :] = tiles[i * 8 : i * 8 + 8]
        for a in range(NQ):
            node = c * PADDED + a * NQ
            low, high = join_rows(load(res, node), load(res, node + ORDER))
            store(res, node, low)
            store(res, node + ORDER, high)
        nodes = range(NODES)
        if c == 0:
            zero = jnp.zeros((8, 128), jnp.float32)
            for side in range(2):
                for b in range(NQ):
                    node = edge_rows[side] * NQ + b
                    sent[0, c, side, b] = -load(res, node)
                    store(res, node, zero)
                    direction[node] = zero
                    out[node] = zero
                start_face(0, c, side)
            nodes = range(NQ, NODES - NQ)
        for i in nodes:
            value = inverse[i] * load(res, c * PADDED + i) * CHEBYSHEV[0][1]
            direction[c * PADDED + i] = value
            out[c * PADDED + i] = value
        prepare_edges(c)

    def update(base, node, change, keep, gain):
        now = load(res, base + node) - change
        store(res, base + node, now)
        value = keep * direction[base + node] + gain * (inverse[node] * now)
        direction[base + node] = value
        out[base + node] += value

    def finish_faces(step, c):
        keep, gain = coefficients(step)
        for side in range(2):
            wait_face(step, c, side)
            for b in range(NQ):
                change = sent[step, c, side, b] + got[step, c, side, b]
                update(c * PADDED, edge_rows[side] * NQ + b, change, keep, gain)

    def prepare_edges(c):
        for b in range(NQ):
            vals = [direction[c * PADDED + a * NQ + b] for a in range(1, ORDER)]
            edges[c * 2 * NQ + b], edges[c * 2 * NQ + NQ + b] = edge_lines([None] + vals + [None])

    def send_edges(step, c):
        base = c * PADDED
        own, across = float(SCALED[0, 0]), float(SCALED[0, ORDER])
        for side in range(2):
            node = edge_rows[side] * NQ
            other = edge_rows[1 - side] * NQ
            vals = [direction[base + node + b] for b in range(NQ)]
            terms = lines(vals, SCALED, 1)
            for b in range(NQ):
                first = edges[c * 2 * NQ + side * NQ + b] + direction[base + other + b] * across
                terms[b] = terms[b] + first + vals[b] * (coeff[node + b] + own)
            terms[0], terms[ORDER] = join_rows(terms[0], terms[ORDER])
            for b in range(NQ):
                sent[step, c, side, b] = terms[b]
            start_face(step, c, side)

    def interior(step, c):
        base = c * PADDED
        keep, gain = coefficients(step)

        def along_first(b, _):
            vals = [direction[base + a * NQ + b] for a in range(NQ)]
            terms = lines(vals, SCALED, 1)
            for a in range(1, ORDER):
                tmp[a * NQ + b] = terms[a] + coeff[a * NQ + b] * vals[a]
            return 0

        def along_second(a, _):
            terms = lines([direction[base + a * NQ + b] for b in range(NQ)], SCALED, 1)
            terms = [terms[b] + tmp[a * NQ + b] for b in range(NQ)]
            terms[0], terms[ORDER] = join_rows(terms[0], terms[ORDER])
            for b in range(NQ):
                update(base, a * NQ + b, terms[b], keep, gain)
            return 0

        lax.fori_loop(0, NQ, along_first, 0, unroll=UNROLL)
        lax.fori_loop(1, ORDER, along_second, 0, unroll=UNROLL)
        prepare_edges(c)

    def sweep(q, _):
        step, c = q // COMPS, q % COMPS
        finish_faces(step, c)
        send_edges(step + 1, c)
        interior(step + 1, c)
        return 0

    begin(0)
    finish_faces(0, 0)
    for c in range(COMPS):
        send_edges(1, c)
        interior(1, c)
        if c + 1 < COMPS:
            begin(c + 1)
    lax.fori_loop(COMPS, (ITERS - 1) * COMPS, sweep, 0)
    saves = []
    for c in range(COMPS):
        finish_faces(ITERS - 1, c)
        part = pl.ds(c * PADDED, NODES)
        saves.append(pltpu.make_async_copy(out.at[part], result.at[part], out_sem.at[c]))
        saves[-1].start()

    for c in range(COMPS):
        saves[c].wait()
        for offset in range(1, OWNERS):
            mode_copy(c, offset).wait_send()
    for side in range(2):

        @pl.when(has[side])
        def _():
            pen_copy(side).wait_send()
            for step in range(ITERS):
                for c in range(COMPS):
                    face_copy(step, c, side).wait_send()


def load(ref, node):
    return ref[pl.ds(pl.multiple_of(node * 8, 8), 8), :]


def store(ref, node, value):
    ref[pl.ds(pl.multiple_of(node * 8, 8), 8), :] = value


def run_step(velocity, penalty):
    tiles = velocity.reshape(COMPS * NODES, 2, 4, 128).transpose(0, 2, 1, 3)
    tiles = tiles.reshape(COMPS * NODES, 8, 128)
    high, low = dft_table()
    pen = penalty.reshape(NODES, 1, 32)
    tile = (8, 128)
    return pl.pallas_call(
        step_kernel,
        out_shape=jax.ShapeDtypeStruct((COMPS * PADDED,) + tile, jnp.float32),
        in_specs=[pl.BlockSpec(memory_space=pltpu.HBM)] * 4,
        out_specs=pl.BlockSpec(memory_space=pltpu.HBM),
        scratch_shapes=[
            pltpu.VMEM((COMPS * PADDED,) + tile, jnp.float32),
            pltpu.VMEM((COMPS * NODES,) + tile, jnp.float32),
            pltpu.VMEM((PLANES, PLANES), jnp.bfloat16),
            pltpu.VMEM((PLANES, PLANES), jnp.bfloat16),
            pltpu.VMEM((NODES, 1, 32), jnp.float32),
            pltpu.VMEM((PADDED, 128), jnp.float32),
            pltpu.VMEM((COMPS * 2 * NQ,) + tile, jnp.float32),
            pltpu.VMEM((COMPS * PADDED * 8, 128), jnp.float32),
            pltpu.VMEM((COMPS * OWNERS * CHUNK, 128), jnp.float32),
            pltpu.VMEM((COMPS * OWNERS * CHUNK, 128), jnp.float32),
            pltpu.VMEM((COMPS * PADDED * 8, 128), jnp.float32),
            pltpu.VMEM((COMPS * PADDED,) + tile, jnp.float32),
            pltpu.VMEM((PADDED,) + tile, jnp.float32),
            pltpu.VMEM((PADDED,) + tile, jnp.float32),
            pltpu.VMEM((PADDED,) + tile, jnp.float32),
            pltpu.VMEM((ITERS, COMPS, 2, NQ) + tile, jnp.float32),
            pltpu.VMEM((ITERS, COMPS, 2, NQ) + tile, jnp.float32),
            pltpu.VMEM((2, 16, 128), jnp.float32),
            pltpu.VMEM((2, 16, 128), jnp.float32),
            pltpu.SemaphoreType.DMA((COMPS, OWNERS)),
            pltpu.SemaphoreType.DMA((COMPS, OWNERS)),
            pltpu.SemaphoreType.DMA((COMPS,)),
            pltpu.SemaphoreType.DMA((ITERS, COMPS, 2)),
            pltpu.SemaphoreType.DMA((ITERS, COMPS, 2)),
            pltpu.SemaphoreType.DMA((2,)),
            pltpu.SemaphoreType.DMA((2,)),
            pltpu.SemaphoreType.DMA((6,)),
            pltpu.SemaphoreType.DMA((COMPS,)),
        ],
        compiler_params=pltpu.CompilerParams(
            collective_id=0, has_side_effects=True, vmem_limit_bytes=VMEM_LIMIT
        ),
        name="step",
    )(tiles, jnp.asarray(high), jnp.asarray(low), pen)


def unpack_kernel(tiles_in, out, tiles, rows, load_sem, sem):
    loads = []
    for c in range(COMPS):
        part = pl.ds(c * PADDED, NODES)
        loads.append(pltpu.make_async_copy(tiles_in.at[part], tiles.at[part], load_sem.at[c]))
        loads[-1].start()
    size = 8 * COMPS * NODES
    copies = []
    for block in range(4):
        for c in range(COMPS):
            if block == 0:
                loads[c].wait()
            for node in range(NODES):
                tile = tiles[c * PADDED + node]
                if block:
                    tile = roll(tile, -32 * block)
                first = block * size + c * NODES + node
                rows[pl.ds(first, 8, stride=COMPS * NODES), :] = tile[:, :32]
        part = pl.ds(block * size, size)
        copies.append(pltpu.make_async_copy(rows.at[part], out.at[part], sem.at[block]))
        copies[-1].start()
    for copy in copies:
        copy.wait()


def unpack_output(tiles):
    shape = (32 * COMPS * NODES, 32)
    out = pl.pallas_call(
        unpack_kernel,
        out_shape=jax.ShapeDtypeStruct(shape, jnp.float32),
        in_specs=[pl.BlockSpec(memory_space=pltpu.HBM)],
        out_specs=pl.BlockSpec(memory_space=pltpu.HBM),
        scratch_shapes=[
            pltpu.VMEM(tiles.shape, jnp.float32),
            pltpu.VMEM(shape, jnp.float32),
            pltpu.SemaphoreType.DMA((COMPS,)),
            pltpu.SemaphoreType.DMA((4,)),
        ],
        compiler_params=pltpu.CompilerParams(vmem_limit_bytes=VMEM_LIMIT),
        name="unpack",
    )(tiles)
    return out.reshape(32, COMPS, NQ, NQ, 1, 32)


def per_device(velocity, penalty):
    return unpack_output(run_step(velocity, penalty))


def solution(mesh):
    return jax.shard_map(
        per_device,
        mesh=mesh,
        in_specs=(P(None, None, None, "mesh", "mode", None), P(None, None, "mesh", None)),
        out_specs=P("mode", None, None, None, "mesh", None),
        check_vma=False,
    )
```
